32 devices in a mesh: req: 8 (over y, x, core), ctx: 4 (over z).
Axes of the slice: x: 2, y: 2, z: 4, core: 2. Of those that a mesh axis runs over, the one named last changes fastest.
Arguments:
- queries: bfloat16 [128, 8192], P(('req', 'ctx')), parts along dimension 0, may hold values from -15 to 15
- new_keys: bfloat16 [128, 512], P(('req', 'ctx')), parts along dimension 0, may hold values from -9 to 9
- new_values: bfloat16 [128, 512], P(('req', 'ctx')), parts along dimension 0, may hold values from -6 to 6
- cache_keys: bfloat16 [65536, 512], P(('req', 'ctx')), parts along dimension 0, may hold values from -6 to 6
- cache_values: bfloat16 [65536, 512], P(('req', 'ctx')), parts along dimension 0, may hold values from -6 to 6
- cache_length: int32 [8], P('req'), parts along dimension 0, may hold values from 2048 to 8191
- page_table: int32 [512], P('req'), parts along dimension 0, may hold values from 0 to 63, each once
Outputs:
- attended: bfloat16 [128, 8192], P(('req', 'ctx')), parts along dimension 0
The draws below stay inside these ranges and needn't reach their ends.
There are 8 independent parts, one for each index of `req`. The reference program is written for one: setup_inputs(seed, part) draws one part's arguments, and reference() takes and returns one part's arrays. A program takes and returns all parts, laid end to end along the dimension named above; each array names one. Nothing has to cross between parts.
Inputs may be any that keep to these rules, and one draw needn't show every extreme that they name: A permutation: logical page p lies in physical rows page_table[p] * 128 to page_table[p] * 128 + 127.
All inputs are finite; a program needn't handle non-finite values.
Results may differ from the reference program's by a relative error of at most 0.004.
Values may be sent and summed in bfloat16 or wider, within the bound.
A program may use at most 64 MiB of HBM per device.

```python
import jax
import jax.numpy as jnp
from jax import lax

QH = 64
KVH = 4
HD = 128
GROUP = 16
PAGE = 128
NEW = 16
NPAGES = 64
CACHE = 8192


def draw_queries(key, part):
    values = 3.0 * jax.random.normal(jax.random.fold_in(key, 5), (NEW, QH * HD), jnp.float32)
    values = jnp.clip(values, -15.0, 15.0)
    return values.astype(jnp.bfloat16)


def draw_new_keys(key, part):
    values = 1.6 * jax.random.normal(jax.random.fold_in(key, 9), (NEW, KVH * HD), jnp.float32)
    values = jnp.clip(values, -9.0, 9.0)
    return values.astype(jnp.bfloat16)


def block_levels(stream_key, dims, split, smallest, largest):
    level, own = 1.0, jax.random.fold_in(stream_key, 6)
    for axis_at, blocks in split:
        steps = jnp.exp(jax.random.uniform(jax.random.fold_in(own, axis_at), (blocks,), jnp.float32, smallest / len(split), largest / len(split)))
        level = level * jnp.repeat(steps, dims[axis_at] // blocks).reshape([-1 if axis == axis_at else 1 for axis in range(len(dims))])
    return level


def normal_values(stream_key, extent, deviation, reach, split=(), kind=jnp.bfloat16):
    array = deviation * jax.random.normal(stream_key, extent, jnp.float32)
    if split:
        array = array * block_levels(stream_key, extent, split, -0.22, 0.18)
    return jnp.clip(array, -reach, reach).astype(kind)


def setup_inputs(seed: int = 0, part: int = 0) -> dict:
    key_list = jax.random.split(jax.random.key(seed), 8)
    part_keys = jax.random.split(jax.random.fold_in(key_list[7], part), 8)
    queries = draw_queries(jax.random.fold_in(jax.random.fold_in(key_list[7], part), 71), part)
    new_keys = draw_new_keys(jax.random.fold_in(jax.random.fold_in(key_list[7], part), 71), part)
    new_values = normal_values(part_keys[2], (NEW, KVH * HD), 1.0, 6.0, ((0, 4),))
    cache_keys = normal_values(part_keys[3], (CACHE, KVH * HD), 1.0, 6.0, ((0, 4),))
    cache_values = normal_values(part_keys[4], (CACHE, KVH * HD), 1.0, 6.0, ((0, 4),))
    cache_length = jax.random.randint(part_keys[5], (1,), CACHE // 4, CACHE).astype(jnp.int32)
    page_table = jax.random.permutation(part_keys[6], NPAGES).astype(jnp.int32)
    return {"queries": queries, "new_keys": new_keys, "new_values": new_values, "cache_keys": cache_keys, "cache_values": cache_values, "cache_length": cache_length, "page_table": page_table}


floor_score = -1.0e30


def reference(queries, new_keys, new_values, cache_keys, cache_values, cache_length, page_table):
    length = cache_length[0]
    page_count = page_table.shape[0]
    logical = jnp.zeros((page_count,), jnp.int32).at[page_table].set(jnp.arange(page_count, dtype=jnp.int32))
    cache_pos = (logical[:, None] * PAGE + jnp.arange(PAGE, dtype=jnp.int32)[None, :]).reshape(-1)
    new_pos = length + jnp.arange(NEW, dtype=jnp.int32)
    key_pos = jnp.concatenate([cache_pos, new_pos])
    key_ok = jnp.concatenate([cache_pos < length, jnp.ones((NEW,), bool)])
    allowed = key_ok[None, :] & (key_pos[None, :] <= new_pos[:, None])
    keys = jnp.concatenate([cache_keys, new_keys], 0).reshape(-1, KVH, HD).transpose(1, 0, 2)
    values = jnp.concatenate([cache_values, new_values], 0).reshape(-1, KVH, HD).transpose(1, 0, 2)
    grouped = queries.reshape(NEW, KVH, GROUP, HD).transpose(1, 0, 2, 3)
    scale = HD ** -0.5

    def one_group(operands):
        query_group, key_group, value_group = operands
        scores = jnp.einsum('qgd,nd->qgn', query_group.astype(jnp.float32), key_group.astype(jnp.float32)) * scale
        scores = jnp.where(allowed[:, None, :], scores, floor_score)
        top = jnp.max(scores, axis=2, keepdims=True)
        weights = jnp.where(allowed[:, None, :], jnp.exp(scores - top), 0.0)
        denominator = jnp.sum(weights, axis=2)
        rounded = lax.optimization_barrier(weights.astype(jnp.bfloat16))
        mixed = jnp.einsum('qgn,nd->qgd', rounded.astype(jnp.float32), value_group.astype(jnp.float32))
        return mixed / denominator[..., None]

    result = lax.map(one_group, (grouped, keys, values))
    return result.transpose(1, 0, 2, 3).reshape(NEW, QH * HD).astype(jnp.bfloat16)
```

```python
import functools
import math

import jax
import jax.numpy as jnp
from jax import lax
from jax.experimental import pallas as pl
from jax.experimental.pallas import tpu as pltpu
from jax.sharding import PartitionSpec as P

HD = 128
PAGE = 128
FLOOR = -1e30
BLOCK = 256


def kernel(
    count,
    q_ref,
    new_k_ref,
    new_v_ref,
    cache_k_ref,
    cache_v_ref,
    length_ref,
    table_ref,
    out_ref,
    new_k,
    new_v,
    length_at,
    table,
    tail,
    q_all,
    k_buf,
    v_buf,
    bias,
    scores,
    part,
    stat,
    part_in,
    stat_in,
    weigh,
    small_sem,
    k_sem,
    v_sem,
    q_send,
    q_recv,
    part_send,
    part_recv,
    stat_send,
    stat_recv,
):
    me = lax.axis_index("ctx")
    kvh, own, _ = q_ref.shape
    rows = new_k_ref.shape[1]
    cached = cache_k_ref.shape[0]
    pages = cached // PAGE
    total_rows = count * own
    block = min(BLOCK, total_rows)
    scale = HD ** (-0.5) * math.log2(math.e)

    def cache_copy(source, target, sems, k):
        return pltpu.make_async_copy(
            source.at[:, pl.ds(k * HD, HD)], target.at[k, pl.ds(0, cached)], sems.at[k]
        )

    barrier = pltpu.get_barrier_semaphore()
    for off in range(1, count):
        pl.semaphore_signal(
            barrier,
            inc=1,
            device_id={"ctx": lax.rem(me + off, count)},
            device_id_type=pl.DeviceIdType.MESH,
        )
    small = [
        pltpu.make_async_copy(source, target, small_sem.at[i])
        for i, (source, target) in enumerate(
            (
                (new_k_ref, new_k),
                (new_v_ref, new_v),
                (length_ref, length_at),
                (table_ref, table),
            )
        )
    ]
    own_q = pltpu.make_async_copy(q_ref, q_all.at[:, me], small_sem.at[len(small)])
    for copy in small:
        copy.start()
    own_q.start()
    for k in range(kvh):
        cache_copy(cache_k_ref, k_buf, k_sem, k).start()
        cache_copy(cache_v_ref, v_buf, v_sem, k).start()
    pl.semaphore_wait(barrier, count - 1)

    def q_copy(k, off):
        return pltpu.make_async_remote_copy(
            src_ref=q_ref.at[k],
            dst_ref=q_all.at[k, me],
            send_sem=q_send.at[k, off - 1],
            recv_sem=q_recv.at[k, off - 1],
            device_id={"ctx": lax.rem(me + off, count)},
            device_id_type=pl.DeviceIdType.MESH,
        )

    def part_copy(k, off):
        target = lax.rem(me + off, count)
        return pltpu.make_async_remote_copy(
            src_ref=part.at[k, target],
            dst_ref=part_in.at[k, me],
            send_sem=part_send.at[k, off - 1],
            recv_sem=part_recv.at[k, off - 1],
            device_id={"ctx": target},
            device_id_type=pl.DeviceIdType.MESH,
        )

    def stat_copy(k, off):
        target = lax.rem(me + off, count)
        return pltpu.make_async_remote_copy(
            src_ref=stat.at[k, target],
            dst_ref=stat_in.at[k, me],
            send_sem=stat_send.at[k, off - 1],
            recv_sem=stat_recv.at[k, off - 1],
            device_id={"ctx": target},
            device_id_type=pl.DeviceIdType.MESH,
        )

    for k in range(kvh):
        for off in range(1, count):
            q_copy(k, off).start()

    for copy in small:
        copy.wait()
    tail[...] = jnp.zeros_like(tail)
    for k in range(kvh):
        tail[0:rows, :] = new_k[k].astype(jnp.float32)
        k_buf[k, cached:, :] = tail[...].astype(jnp.bfloat16)
        tail[0:rows, :] = new_v[k].astype(jnp.float32)
        v_buf[k, cached:, :] = tail[...].astype(jnp.bfloat16)

    length = length_at[0]
    slots = me * pages + lax.broadcasted_iota(jnp.int32, (pages, table.shape[1]), 0)
    order = lax.broadcasted_iota(jnp.int32, (pages, table.shape[1]), 1)
    hits = jnp.where(table[...] == slots, order, 0)
    logical = jnp.sum(hits, axis=1, keepdims=True)
    lane = lax.broadcasted_iota(jnp.int32, (pages, PAGE), 1)
    bias[...] = jnp.where(logical * PAGE + lane < length, 0.0, FLOOR)

    spans = [(at, min(BLOCK, cached - at)) for at in range(0, cached, BLOCK)]

    def attend(k, at):
        if total_rows == block:
            query = q_all[k].reshape(total_rows, HD)
        else:
            parts = block // own
            query = q_all[k, pl.ds(at * parts, parts)].reshape(block, HD)
        top = None
        for start, size in spans:
            score = lax.dot_general(
                query,
                k_buf[k, start : start + size, :],
                (((1,), (1,)), ((), ())),
                preferred_element_type=jnp.float32,
            )
            for page in range(size // PAGE):
                j = start // PAGE + page
                tile = score[:, page * PAGE : (page + 1) * PAGE] * scale + bias[j : j + 1, :]
                scores[:, j * PAGE : (j + 1) * PAGE] = tile
                top = tile if top is None else jnp.maximum(top, tile)
        score = lax.dot_general(
            query,
            k_buf[k, cached:, :],
            (((1,), (1,)), ((), ())),
            preferred_element_type=jnp.float32,
        )
        row = at * block + lax.broadcasted_iota(jnp.int32, (block, PAGE), 0)
        column = lax.broadcasted_iota(jnp.int32, (block, PAGE), 1)
        token = (row // own) * rows + row % rows
        allowed = (column < rows) & (me * rows + column <= token)
        last = jnp.where(allowed, score * scale, FLOOR)
        top = jnp.max(jnp.maximum(top, last), axis=1, keepdims=True)
        weight = jnp.exp2(last - top)
        summed = weight
        mixed = jnp.dot(
            weight.astype(jnp.bfloat16), v_buf[k, cached:, :], preferred_element_type=jnp.float32
        )
        for start, size in spans:
            weight = jnp.exp2(scores[:, start : start + size] - top)
            for page in range(size // PAGE):
                summed = summed + weight[:, page * PAGE : (page + 1) * PAGE]
            mixed = mixed + jnp.dot(
                weight.astype(jnp.bfloat16),
                v_buf[k, start : start + size, :],
                preferred_element_type=jnp.float32,
            )
        total = jnp.sum(summed, axis=1, keepdims=True)
        mixed = mixed * (1.0 / total)
        lanes = lax.broadcasted_iota(jnp.int32, (2 * own, 128), 1)
        columns = jnp.zeros((2 * own, 128), jnp.float32)
        for i in range(block // own):
            piece = slice(i * own, (i + 1) * own)
            slot = at * (block // own) + i
            part[k, slot] = mixed[piece].astype(jnp.bfloat16)
            column = jnp.concatenate([top[piece], total[piece]], axis=0)
            columns = jnp.where(lanes == i, column, columns)
        turned = columns.T
        for i in range(block // own):
            stat[k, at * (block // own) + i] = turned[i : i + 1, :]

    own_q.wait()

    def one_head(k, carry):
        for off in range(1, count):
            q_copy(k, off).wait_recv()
        cache_copy(cache_k_ref, k_buf, k_sem, k).wait()
        cache_copy(cache_v_ref, v_buf, v_sem, k).wait()
        if total_rows == block:
            attend(k, 0)
        else:
            lax.fori_loop(0, total_rows // block, lambda at, c: (attend(k, at), c)[1], 0)
        for off in range(1, count):
            part_copy(k, off).start()
            stat_copy(k, off).start()
        part_in[k, me] = part[k, me]
        stat_in[k, me] = stat[k, me]
        return carry

    lax.fori_loop(0, kvh, one_head, 0)

    def combine(k, carry):
        for off in range(1, count):
            part_copy(k, off).wait_recv()
            stat_copy(k, off).wait_recv()
        tops = [stat_in[k, s] for s in range(count)]
        totals = [pltpu.roll(t, own, 1) for t in tops]
        top = functools.reduce(jnp.maximum, tops)
        shares = [jnp.exp2(t - top) * l for t, l in zip(tops, totals)]
        share = 1.0 / functools.reduce(jnp.add, shares)
        for s in range(count):
            weigh[s : s + 1, :] = shares[s] * share
        turned = weigh[...].T
        result = jnp.zeros((own, HD), jnp.float32)
        for s in range(count):
            result = result + part_in[k, s].astype(jnp.float32) * turned[0:own, s : s + 1]
        out_ref[k] = result.astype(out_ref.dtype)
        return carry

    weigh[...] = jnp.zeros_like(weigh)
    lax.fori_loop(0, kvh, combine, 0)

    for k in range(kvh):
        for off in range(1, count):
            q_copy(k, off).wait_send()
            part_copy(k, off).wait_send()
            stat_copy(k, off).wait_send()


def local(queries, new_keys, new_values, cache_keys, cache_values, cache_length, page_table):
    count = lax.axis_size("ctx")
    rows, width = queries.shape
    heads = width // HD
    cached = cache_keys.shape[0]
    kvh = cache_keys.shape[1] // HD
    group = heads // kvh
    own = rows * group
    block = min(BLOCK, count * own)
    pages = cached // PAGE
    vmem = pl.BlockSpec(memory_space=pltpu.VMEM)
    held = pl.BlockSpec(memory_space=pl.ANY)
    dma = pltpu.SemaphoreType.DMA
    out = pl.pallas_call(
        functools.partial(kernel, count),
        out_shape=jax.ShapeDtypeStruct((kvh, own, HD), jnp.bfloat16),
        in_specs=[held] * 7,
        out_specs=vmem,
        scratch_shapes=[
            pltpu.VMEM((kvh, rows, HD), jnp.bfloat16),
            pltpu.VMEM((kvh, rows, HD), jnp.bfloat16),
            pltpu.SMEM((1,), jnp.int32),
            pltpu.VMEM((1, page_table.shape[0]), jnp.int32),
            pltpu.VMEM((PAGE, HD), jnp.float32),
            pltpu.VMEM((kvh, count, own, HD), jnp.bfloat16),
            pltpu.VMEM((kvh, cached + PAGE, HD), jnp.bfloat16),
            pltpu.VMEM((kvh, cached + PAGE, HD), jnp.bfloat16),
            pltpu.VMEM((pages, PAGE), jnp.float32),
            pltpu.VMEM((block, cached), jnp.float32),
            pltpu.VMEM((kvh, count, own, HD), jnp.bfloat16),
            pltpu.VMEM((kvh, count, 1, 2 * own), jnp.float32),
            pltpu.VMEM((kvh, count, own, HD), jnp.bfloat16),
            pltpu.VMEM((kvh, count, 1, 2 * own), jnp.float32),
            pltpu.VMEM((128, 2 * own), jnp.float32),
            dma((5,)),
            dma((kvh,)),
            dma((kvh,)),
            dma((kvh, count - 1)),
            dma((kvh, count - 1)),
            dma((kvh, count - 1)),
            dma((kvh, count - 1)),
            dma((kvh, count - 1)),
            dma((kvh, count - 1)),
        ],
        compiler_params=pltpu.CompilerParams(
            collective_id=0, has_side_effects=True, vmem_limit_bytes=60 * 1024 * 1024
        ),
        cost_estimate=pl.CostEstimate(
            flops=4 * count * rows * heads * cached * HD,
            bytes_accessed=4 * cached * kvh * HD,
            transcendentals=count * rows * heads * cached,
        ),
        name="paged_attention",
    )(
        queries.reshape(rows, heads, HD).transpose(1, 0, 2).reshape(kvh, own, HD),
        new_keys.reshape(rows, kvh, HD).transpose(1, 0, 2),
        new_values.reshape(rows, kvh, HD).transpose(1, 0, 2),
        cache_keys,
        cache_values,
        cache_length,
        page_table.reshape(1, -1),
    )
    return out.reshape(heads, rows, HD).transpose(1, 0, 2).reshape(rows, width)


def solution(mesh):
    in_specs = (
        P(("req", "ctx"), None),
        P(("req", "ctx"), None),
        P(("req", "ctx"), None),
        P(("req", "ctx"), None),
        P(("req", "ctx"), None),
        P("req"),
        P("req"),
    )
    out_specs = P(("req", "ctx"), None)
    return jax.shard_map(local, mesh=mesh, in_specs=in_specs, out_specs=out_specs, check_vma=False)
```

```python
import functools
import math

import jax
import jax.numpy as jnp
from jax import lax
from jax.experimental import pallas as pl
from jax.experimental.pallas import tpu as pltpu
from jax.sharding import PartitionSpec as P

HD = 128
PAGE = 128
FLOOR = -1e30
BLOCK = 256


def kernel(
    count,
    q_ref,
    new_k_ref,
    new_v_ref,
    cache_k_ref,
    cache_v_ref,
    length_ref,
    table_ref,
    out_ref,
    new_k,
    new_v,
    length_at,
    table,
    tail,
    q_all,
    k_buf,
    v_buf,
    bias,
    scores,
    part,
    stat,
    part_in,
    stat_in,
    weigh,
    small_sem,
    k_sem,
    v_sem,
    q_send,
    q_recv,
    part_send,
    part_recv,
    stat_send,
    stat_recv,
):
    me = lax.axis_index("ctx")
    kvh, own, _ = q_ref.shape
    rows = new_k_ref.shape[1]
    cached = cache_k_ref.shape[0]
    pages = cached // PAGE
    total_rows = count * own
    block = min(BLOCK, total_rows)
    scale = HD ** (-0.5) * math.log2(math.e)

    def cache_copy(source, target, sems, k):
        return pltpu.make_async_copy(
            source.at[:, pl.ds(k * HD, HD)], target.at[k, pl.ds(0, cached)], sems.at[k]
        )

    barrier = pltpu.get_barrier_semaphore()
    for off in range(1, count):
        pl.semaphore_signal(
            barrier,
            inc=1,
            device_id={"ctx": lax.rem(me + off, count)},
            device_id_type=pl.DeviceIdType.MESH,
        )
    small = [
        pltpu.make_async_copy(source, target, small_sem.at[i])
        for i, (source, target) in enumerate(
            (
                (new_k_ref, new_k),
                (new_v_ref, new_v),
                (length_ref, length_at),
                (table_ref, table),
            )
        )
    ]
    own_q = pltpu.make_async_copy(q_ref, q_all.at[:, me], small_sem.at[len(small)])
    for copy in small:
        copy.start()
    own_q.start()
    for k in range(kvh):
        cache_copy(cache_k_ref, k_buf, k_sem, k).start()
        cache_copy(cache_v_ref, v_buf, v_sem, k).start()
    pl.semaphore_wait(barrier, count - 1)

    def q_copy(k, off):
        return pltpu.make_async_remote_copy(
            src_ref=q_ref.at[k],
            dst_ref=q_all.at[k, me],
            send_sem=q_send.at[k, off - 1],
            recv_sem=q_recv.at[k, off - 1],
            device_id={"ctx": lax.rem(me + off, count)},
            device_id_type=pl.DeviceIdType.MESH,
        )

    def part_copy(k, off):
        target = lax.rem(me + off, count)
        return pltpu.make_async_remote_copy(
            src_ref=part.at[k, target],
            dst_ref=part_in.at[k, me],
            send_sem=part_send.at[k, off - 1],
            recv_sem=part_recv.at[k, off - 1],
            device_id={"ctx": target},
            device_id_type=pl.DeviceIdType.MESH,
        )

    def stat_copy(k, off):
        target = lax.rem(me + off, count)
        return pltpu.make_async_remote_copy(
            src_ref=stat.at[k, target],
            dst_ref=stat_in.at[k, me],
            send_sem=stat_send.at[k, off - 1],
            recv_sem=stat_recv.at[k, off - 1],
            device_id={"ctx": target},
            device_id_type=pl.DeviceIdType.MESH,
        )

    for k in range(kvh):
        for off in range(1, count):
            q_copy(k, off).start()

    for copy in small:
        copy.wait()
    tail[...] = jnp.zeros_like(tail)
    for k in range(kvh):
        tail[0:rows, :] = new_k[k].astype(jnp.float32)
        k_buf[k, cached:, :] = tail[...].astype(jnp.bfloat16)
        tail[0:rows, :] = new_v[k].astype(jnp.float32)
        v_buf[k, cached:, :] = tail[...].astype(jnp.bfloat16)

    length = length_at[0]
    slots = me * pages + lax.broadcasted_iota(jnp.int32, (pages, table.shape[1]), 0)
    order = lax.broadcasted_iota(jnp.int32, (pages, table.shape[1]), 1)
    hits = jnp.where(table[...] == slots, order, 0)
    logical = jnp.sum(hits, axis=1, keepdims=True)
    lane = lax.broadcasted_iota(jnp.int32, (pages, PAGE), 1)
    bias[...] = jnp.where(logical * PAGE + lane < length, 0.0, FLOOR)

    spans = [(at, min(BLOCK, cached - at)) for at in range(0, cached, BLOCK)]

    def attend(k, at):
        if total_rows == block:
            query = q_all[k].reshape(total_rows, HD)
        else:
            parts = block // own
            query = q_all[k, pl.ds(at * parts, parts)].reshape(block, HD)
        top = None
        for start, size in spans:
            score = lax.dot_general(
                query,
                k_buf[k, start : start + size, :],
                (((1,), (1,)), ((), ())),
                preferred_element_type=jnp.float32,
            )
            for page in range(size // PAGE):
                j = start // PAGE + page
                tile = score[:, page * PAGE : (page + 1) * PAGE] * scale + bias[j : j + 1, :]
                scores[:, j * PAGE : (j + 1) * PAGE] = tile
                top = tile if top is None else jnp.maximum(top, tile)
        score = lax.dot_general(
            query,
            k_buf[k, cached:, :],
            (((1,), (1,)), ((), ())),
            preferred_element_type=jnp.float32,
        )
        row = at * block + lax.broadcasted_iota(jnp.int32, (block, PAGE), 0)
        column = lax.broadcasted_iota(jnp.int32, (block, PAGE), 1)
        token = (row // own) * rows + row % rows
        allowed = (column < rows) & (me * rows + column <= token)
        last = jnp.where(allowed, score * scale, FLOOR)
        top = jnp.max(jnp.maximum(top, last), axis=1, keepdims=True)
        weight = jnp.exp2(last - top)
        summed = weight
        mixed = jnp.dot(
            weight.astype(jnp.bfloat16), v_buf[k, cached:, :], preferred_element_type=jnp.float32
        )
        for start, size in spans:
            weight = jnp.exp2(scores[:, start : start + size] - top)
            for page in range(size // PAGE):
                summed = summed + weight[:, page * PAGE : (page + 1) * PAGE]
            mixed = mixed + jnp.dot(
                weight.astype(jnp.bfloat16),
                v_buf[k, start : start + size, :],
                preferred_element_type=jnp.float32,
            )
        total = jnp.sum(summed, axis=1, keepdims=True)
        mixed = mixed * (1.0 / total)
        lanes = lax.broadcasted_iota(jnp.int32, (2 * own, 128), 1)
        columns = jnp.zeros((2 * own, 128), jnp.float32)
        for i in range(block // own):
            piece = slice(i * own, (i + 1) * own)
            slot = at * (block // own) + i
            part[k, slot] = mixed[piece].astype(jnp.bfloat16)
            column = jnp.concatenate([top[piece], total[piece]], axis=0)
            columns = jnp.where(lanes == i, column, columns)
        turned = columns.T
        for i in range(block // own):
            stat[k, at * (block // own) + i] = turned[i : i + 1, :]

    own_q.wait()

    def one_head(k, carry):
        for off in range(1, count):
            q_copy(k, off).wait_recv()
        cache_copy(cache_k_ref, k_buf, k_sem, k).wait()
        cache_copy(cache_v_ref, v_buf, v_sem, k).wait()
        if total_rows == block:
            attend(k, 0)
        else:
            lax.fori_loop(0, total_rows // block, lambda at, c: (attend(k, at), c)[1], 0)
        for off in range(1, count):
            part_copy(k, off).start()
            stat_copy(k, off).start()
        part_in[k, me] = part[k, me]
        stat_in[k, me] = stat[k, me]
        return carry

    lax.fori_loop(0, kvh, one_head, 0)

    def combine(k, carry):
        for off in range(1, count):
            part_copy(k, off).wait_recv()
            stat_copy(k, off).wait_recv()
        tops = [stat_in[k, s] for s in range(count)]
        totals = [pltpu.roll(t, own, 1) for t in tops]
        top = functools.reduce(jnp.maximum, tops)
        shares = [jnp.exp2(t - top) * l for t, l in zip(tops, totals)]
        share = 1.0 / functools.reduce(jnp.add, shares)
        for s in range(count):
            weigh[s : s + 1, :] = shares[s] * share
        turned = weigh[...].T
        result = jnp.zeros((own, HD), jnp.float32)
        for s in range(count):
            result = result + part_in[k, s].astype(jnp.float32) * turned[0:own, s : s + 1]
        out_ref[k] = result.astype(out_ref.dtype)
        return carry

    weigh[...] = jnp.zeros_like(weigh)
    lax.fori_loop(0, kvh, combine, 0)

    for k in range(kvh):
        for off in range(1, count):
            q_copy(k, off).wait_send()
            part_copy(k, off).wait_send()
            stat_copy(k, off).wait_send()


def local(queries, new_keys, new_values, cache_keys, cache_values, cache_length, page_table):
    count = lax.axis_size("ctx")
    rows, width = queries.shape
    heads = width // HD
    cached = cache_keys.shape[0]
    kvh = cache_keys.shape[1] // HD
    group = heads // kvh
    own = rows * group
    block = min(BLOCK, count * own)
    pages = cached // PAGE
    vmem = pl.BlockSpec(memory_space=pltpu.VMEM)
    held = pl.BlockSpec(memory_space=pltpu.HBM)
    dma = pltpu.SemaphoreType.DMA
    out = pl.pallas_call(
        functools.partial(kernel, count),
        out_shape=pltpu.VMEM((kvh, own, HD), jnp.bfloat16),
        in_specs=[held] * 7,
        out_specs=vmem,
        scratch_shapes=[
            pltpu.VMEM((kvh, rows, HD), jnp.bfloat16),
            pltpu.VMEM((kvh, rows, HD), jnp.bfloat16),
            pltpu.SMEM((1,), jnp.int32),
            pltpu.VMEM((1, page_table.shape[0]), jnp.int32),
            pltpu.VMEM((PAGE, HD), jnp.float32),
            pltpu.VMEM((kvh, count, own, HD), jnp.bfloat16),
            pltpu.VMEM((kvh, cached + PAGE, HD), jnp.bfloat16),
            pltpu.VMEM((kvh, cached + PAGE, HD), jnp.bfloat16),
            pltpu.VMEM((pages, PAGE), jnp.float32),
            pltpu.VMEM((block, cached), jnp.float32),
            pltpu.VMEM((kvh, count, own, HD), jnp.bfloat16),
            pltpu.VMEM((kvh, count, 1, 2 * own), jnp.float32),
            pltpu.VMEM((kvh, count, own, HD), jnp.bfloat16),
            pltpu.VMEM((kvh, count, 1, 2 * own), jnp.float32),
            pltpu.VMEM((128, 2 * own), jnp.float32),
            dma((5,)),
            dma((kvh,)),
            dma((kvh,)),
            dma((kvh, count - 1)),
            dma((kvh, count - 1)),
            dma((kvh, count - 1)),
            dma((kvh, count - 1)),
            dma((kvh, count - 1)),
            dma((kvh, count - 1)),
        ],
        compiler_params=pltpu.CompilerParams(
            collective_id=0, has_side_effects=True, vmem_limit_bytes=60 * 1024 * 1024
        ),
        cost_estimate=pl.CostEstimate(
            flops=4 * count * rows * heads * cached * HD,
            bytes_accessed=4 * cached * kvh * HD,
            transcendentals=count * rows * heads * cached,
        ),
        name="paged_attention",
    )(
        queries.reshape(rows, heads, HD).transpose(1, 0, 2).reshape(kvh, own, HD),
        new_keys.reshape(rows, kvh, HD).transpose(1, 0, 2),
        new_values.reshape(rows, kvh, HD).transpose(1, 0, 2),
        cache_keys,
        cache_values,
        cache_length,
        page_table.reshape(1, -1),
    )
    return out.reshape(heads, rows, HD).transpose(1, 0, 2).reshape(rows, width)


def solution(mesh):
    in_specs = (
        P(("req", "ctx"), None),
        P(("req", "ctx"), None),
        P(("req", "ctx"), None),
        P(("req", "ctx"), None),
        P(("req", "ctx"), None),
        P("req"),
        P("req"),
    )
    out_specs = P(("req", "ctx"), None)
    return jax.shard_map(local, mesh=mesh, in_specs=in_specs, out_specs=out_specs, check_vma=False)
```

```python
import functools
import math

import jax
import jax.numpy as jnp
from jax import lax
from jax.experimental import pallas as pl
from jax.experimental.pallas import tpu as pltpu
from jax.sharding import PartitionSpec as P

HD = 128
PAGE = 128
FLOOR = -1e30
BLOCK = 256


def kernel(
    count,
    q_ref,
    new_k_ref,
    new_v_ref,
    cache_k_ref,
    cache_v_ref,
    length_ref,
    table_ref,
    out_ref,
    new_k,
    new_v,
    length_at,
    table,
    tail,
    q_all,
    k_buf,
    v_buf,
    bias,
    scores,
    part,
    stat,
    part_in,
    stat_in,
    weigh,
    small_sem,
    k_sem,
    v_sem,
    q_send,
    q_recv,
    cross_send,
    cross_recv,
    pass_send,
    pass_recv,
    part_send,
    part_recv,
    stat_send,
    stat_recv,
):
    me = lax.axis_index("ctx")
    kvh, own, _ = q_ref.shape
    rows = new_k_ref.shape[1]
    cached = cache_k_ref.shape[0]
    pages = cached // PAGE
    total_rows = count * own
    block = min(BLOCK, total_rows)
    scale = HD ** (-0.5) * math.log2(math.e)

    def cache_copy(source, target, sems, k):
        return pltpu.make_async_copy(
            source.at[:, pl.ds(k * HD, HD)], target.at[k, pl.ds(0, cached)], sems.at[k]
        )

    barrier = pltpu.get_barrier_semaphore()
    for off in range(1, count):
        pl.semaphore_signal(
            barrier,
            inc=1,
            device_id={"ctx": lax.rem(me + off, count)},
            device_id_type=pl.DeviceIdType.MESH,
        )
    small = [
        pltpu.make_async_copy(source, target, small_sem.at[i])
        for i, (source, target) in enumerate(
            (
                (new_k_ref, new_k),
                (new_v_ref, new_v),
                (length_ref, length_at),
                (table_ref, table),
            )
        )
    ]
    own_q = pltpu.make_async_copy(q_ref, q_all.at[:, me], small_sem.at[len(small)])
    for copy in small:
        copy.start()
    own_q.start()
    for k in range(kvh):
        cache_copy(cache_k_ref, k_buf, k_sem, k).start()
        cache_copy(cache_v_ref, v_buf, v_sem, k).start()
    pl.semaphore_wait(barrier, count - 1)

    halves = 2 if count % 2 == 0 else 1
    half = count // halves
    side = me // half
    base = side * half
    other = (halves - 1 - side) * half
    relay = me == half - 1 + side

    def near(off):
        return base + lax.rem(me - base + off, half)

    def q_copy(k, off):
        return pltpu.make_async_remote_copy(
            src_ref=q_ref.at[k],
            dst_ref=q_all.at[k, me],
            send_sem=q_send.at[k, off - 1],
            recv_sem=q_recv.at[k, off - 1],
            device_id={"ctx": near(off)},
            device_id_type=pl.DeviceIdType.MESH,
        )

    def cross_copy(k, slot):
        return pltpu.make_async_remote_copy(
            src_ref=q_ref.at[k],
            dst_ref=q_all.at[k, me],
            send_sem=cross_send.at[k],
            recv_sem=cross_recv.at[k, slot],
            device_id={"ctx": half - side},
            device_id_type=pl.DeviceIdType.MESH,
        )

    def pass_copy(k, off):
        return pltpu.make_async_remote_copy(
            src_ref=q_all.at[k, pl.ds(other, half)],
            dst_ref=q_all.at[k, pl.ds(other, half)],
            send_sem=pass_send.at[k, off - 1],
            recv_sem=pass_recv.at[k],
            device_id={"ctx": near(off)},
            device_id_type=pl.DeviceIdType.MESH,
        )

    def pass_on(k):
        for slot in range(half):
            cross_copy(k, slot).wait_recv()
        for off in range(1, half):
            pass_copy(k, off).start()

    def part_copy(k, off):
        target = lax.rem(me + off, count)
        return pltpu.make_async_remote_copy(
            src_ref=part.at[k, target],
            dst_ref=part_in.at[k, me],
            send_sem=part_send.at[k, off - 1],
            recv_sem=part_recv.at[k, off - 1],
            device_id={"ctx": target},
            device_id_type=pl.DeviceIdType.MESH,
        )

    def stat_copy(k, off):
        target = lax.rem(me + off, count)
        return pltpu.make_async_remote_copy(
            src_ref=stat.at[k, target],
            dst_ref=stat_in.at[k, me],
            send_sem=stat_send.at[k, off - 1],
            recv_sem=stat_recv.at[k, off - 1],
            device_id={"ctx": target},
            device_id_type=pl.DeviceIdType.MESH,
        )

    for k in range(kvh):
        if halves == 2:
            cross_copy(k, me - base).start()
        for off in range(1, half):
            q_copy(k, off).start()

    for copy in small:
        copy.wait()
    tail[...] = jnp.zeros_like(tail)
    for k in range(kvh):
        tail[0:rows, :] = new_k[k].astype(jnp.float32)
        k_buf[k, cached:, :] = tail[...].astype(jnp.bfloat16)
        tail[0:rows, :] = new_v[k].astype(jnp.float32)
        v_buf[k, cached:, :] = tail[...].astype(jnp.bfloat16)

    length = length_at[0]
    slots = me * pages + lax.broadcasted_iota(jnp.int32, (pages, table.shape[1]), 0)
    order = lax.broadcasted_iota(jnp.int32, (pages, table.shape[1]), 1)
    hits = jnp.where(table[...] == slots, order, 0)
    logical = jnp.sum(hits, axis=1, keepdims=True)
    lane = lax.broadcasted_iota(jnp.int32, (pages, PAGE), 1)
    bias[...] = jnp.where(logical * PAGE + lane < length, 0.0, FLOOR)

    spans = [(at, min(BLOCK, cached - at)) for at in range(0, cached, BLOCK)]

    def attend(k, at, between=None):
        if total_rows == block:
            query = q_all[k].reshape(total_rows, HD)
        else:
            parts = block // own
            query = q_all[k, pl.ds(at * parts, parts)].reshape(block, HD)
        top = None
        for start, size in spans:
            score = lax.dot_general(
                query,
                k_buf[k, start : start + size, :],
                (((1,), (1,)), ((), ())),
                preferred_element_type=jnp.float32,
            )
            for page in range(size // PAGE):
                j = start // PAGE + page
                tile = score[:, page * PAGE : (page + 1) * PAGE] * scale + bias[j : j + 1, :]
                scores[:, j * PAGE : (j + 1) * PAGE] = tile
                top = tile if top is None else jnp.maximum(top, tile)
        score = lax.dot_general(
            query,
            k_buf[k, cached:, :],
            (((1,), (1,)), ((), ())),
            preferred_element_type=jnp.float32,
        )
        if between is not None:
            between()
        row = at * block + lax.broadcasted_iota(jnp.int32, (block, PAGE), 0)
        column = lax.broadcasted_iota(jnp.int32, (block, PAGE), 1)
        token = (row // own) * rows + row % rows
        allowed = (column < rows) & (me * rows + column <= token)
        last = jnp.where(allowed, score * scale, FLOOR)
        top = jnp.max(jnp.maximum(top, last), axis=1, keepdims=True)
        weight = jnp.exp2(last - top)
        summed = weight
        mixed = jnp.dot(
            weight.astype(jnp.bfloat16), v_buf[k, cached:, :], preferred_element_type=jnp.float32
        )
        for start, size in spans:
            weight = jnp.exp2(scores[:, start : start + size] - top)
            for page in range(size // PAGE):
                summed = summed + weight[:, page * PAGE : (page + 1) * PAGE]
            mixed = mixed + jnp.dot(
                weight.astype(jnp.bfloat16),
                v_buf[k, start : start + size, :],
                preferred_element_type=jnp.float32,
            )
        total = jnp.sum(summed, axis=1, keepdims=True)
        mixed = mixed * (1.0 / total)
        lanes = lax.broadcasted_iota(jnp.int32, (2 * own, 128), 1)
        columns = jnp.zeros((2 * own, 128), jnp.float32)
        for i in range(block // own):
            piece = slice(i * own, (i + 1) * own)
            slot = at * (block // own) + i
            part[k, slot] = mixed[piece].astype(jnp.bfloat16)
            column = jnp.concatenate([top[piece], total[piece]], axis=0)
            columns = jnp.where(lanes == i, column, columns)
        turned = columns.T
        for i in range(block // own):
            stat[k, at * (block // own) + i] = turned[i : i + 1, :]

    own_q.wait()
    if halves == 2:
        pl.when(relay)(lambda: pass_on(0))

    def pass_next(k):
        if halves == 2:
            pl.when(relay & (k + 1 < kvh))(lambda: pass_on(k + 1))

    def one_head(k, carry):
        for off in range(1, half):
            q_copy(k, off).wait_recv()
        if halves == 2 and half > 1:

            @pl.when(jnp.logical_not(relay))
            def _():
                pass_copy(k, 1).wait_recv()

        cache_copy(cache_k_ref, k_buf, k_sem, k).wait()
        cache_copy(cache_v_ref, v_buf, v_sem, k).wait()
        if total_rows == block:
            attend(k, 0, lambda: pass_next(k))
        else:
            pass_next(k)
            lax.fori_loop(0, total_rows // block, lambda at, c: (attend(k, at), c)[1], 0)
        for off in range(1, count):
            part_copy(k, off).start()
            stat_copy(k, off).start()
        part_in[k, me] = part[k, me]
        stat_in[k, me] = stat[k, me]
        return carry

    lax.fori_loop(0, kvh, one_head, 0)

    def combine(k, carry):
        for off in range(1, count):
            part_copy(k, off).wait_recv()
            stat_copy(k, off).wait_recv()
        tops = [stat_in[k, s] for s in range(count)]
        totals = [pltpu.roll(t, own, 1) for t in tops]
        top = functools.reduce(jnp.maximum, tops)
        shares = [jnp.exp2(t - top) * l for t, l in zip(tops, totals)]
        share = 1.0 / functools.reduce(jnp.add, shares)
        for s in range(count):
            weigh[s : s + 1, :] = shares[s] * share
        turned = weigh[...].T
        result = jnp.zeros((own, HD), jnp.float32)
        for s in range(count):
            result = result + part_in[k, s].astype(jnp.float32) * turned[0:own, s : s + 1]
        out_ref[k] = result.astype(out_ref.dtype)
        return carry

    weigh[...] = jnp.zeros_like(weigh)
    lax.fori_loop(0, kvh, combine, 0)

    for k in range(kvh):
        for off in range(1, half):
            q_copy(k, off).wait_send()
        for off in range(1, count):
            part_copy(k, off).wait_send()
            stat_copy(k, off).wait_send()
    if halves == 2:
        for k in range(kvh):
            cross_copy(k, 0).wait_send()

        @pl.when(relay)
        def _():
            for k in range(kvh):
                for off in range(1, half):
                    pass_copy(k, off).wait_send()


def local(queries, new_keys, new_values, cache_keys, cache_values, cache_length, page_table):
    count = lax.axis_size("ctx")
    rows, width = queries.shape
    heads = width // HD
    cached = cache_keys.shape[0]
    kvh = cache_keys.shape[1] // HD
    group = heads // kvh
    own = rows * group
    block = min(BLOCK, count * own)
    pages = cached // PAGE
    half = count // 2 if count % 2 == 0 else count
    vmem = pl.BlockSpec(memory_space=pltpu.VMEM)
    held = pl.BlockSpec(memory_space=pltpu.HBM)
    dma = pltpu.SemaphoreType.DMA
    out = pl.pallas_call(
        functools.partial(kernel, count),
        out_shape=pltpu.VMEM((kvh, own, HD), jnp.bfloat16),
        in_specs=[held] * 7,
        out_specs=vmem,
        scratch_shapes=[
            pltpu.VMEM((kvh, rows, HD), jnp.bfloat16),
            pltpu.VMEM((kvh, rows, HD), jnp.bfloat16),
            pltpu.SMEM((1,), jnp.int32),
            pltpu.VMEM((1, page_table.shape[0]), jnp.int32),
            pltpu.VMEM((PAGE, HD), jnp.float32),
            pltpu.VMEM((kvh, count, own, HD), jnp.bfloat16),
            pltpu.VMEM((kvh, cached + PAGE, HD), jnp.bfloat16),
            pltpu.VMEM((kvh, cached + PAGE, HD), jnp.bfloat16),
            pltpu.VMEM((pages, PAGE), jnp.float32),
            pltpu.VMEM((block, cached), jnp.float32),
            pltpu.VMEM((kvh, count, own, HD), jnp.bfloat16),
            pltpu.VMEM((kvh, count, 1, 2 * own), jnp.float32),
            pltpu.VMEM((kvh, count, own, HD), jnp.bfloat16),
            pltpu.VMEM((kvh, count, 1, 2 * own), jnp.float32),
            pltpu.VMEM((128, 2 * own), jnp.float32),
            dma((5,)),
            dma((kvh,)),
            dma((kvh,)),
            dma((kvh, max(half - 1, 1))),
            dma((kvh, max(half - 1, 1))),
            dma((kvh,)),
            dma((kvh, half)),
            dma((kvh, max(half - 1, 1))),
            dma((kvh,)),
            dma((kvh, count - 1)),
            dma((kvh, count - 1)),
            dma((kvh, count - 1)),
            dma((kvh, count - 1)),
        ],
        compiler_params=pltpu.CompilerParams(
            collective_id=0, has_side_effects=True, vmem_limit_bytes=60 * 1024 * 1024
        ),
        cost_estimate=pl.CostEstimate(
            flops=4 * count * rows * heads * cached * HD,
            bytes_accessed=4 * cached * kvh * HD,
            transcendentals=count * rows * heads * cached,
        ),
        name="paged_attention",
    )(
        queries.reshape(rows, heads, HD).transpose(1, 0, 2).reshape(kvh, own, HD),
        new_keys.reshape(rows, kvh, HD).transpose(1, 0, 2),
        new_values.reshape(rows, kvh, HD).transpose(1, 0, 2),
        cache_keys,
        cache_values,
        cache_length,
        page_table.reshape(1, -1),
    )
    return out.reshape(heads, rows, HD).transpose(1, 0, 2).reshape(rows, width)


def solution(mesh):
    in_specs = (
        P(("req", "ctx"), None),
        P(("req", "ctx"), None),
        P(("req", "ctx"), None),
        P(("req", "ctx"), None),
        P(("req", "ctx"), None),
        P("req"),
        P("req"),
    )
    out_specs = P(("req", "ctx"), None)
    return jax.shard_map(local, mesh=mesh, in_specs=in_specs, out_specs=out_specs, check_vma=False)
```

```python
import functools
import math

import jax
import jax.numpy as jnp
from jax import lax
from jax.experimental import pallas as pl
from jax.experimental.pallas import tpu as pltpu
from jax.sharding import PartitionSpec as P

HD = 128
PAGE = 128
FLOOR = -1e30
BLOCK = 256


def kernel(
    count,
    q_ref,
    new_k_ref,
    new_v_ref,
    cache_k_ref,
    cache_v_ref,
    length_ref,
    table_ref,
    out_ref,
    new_k,
    new_v,
    length_at,
    table,
    tail,
    q_all,
    q_mark,
    k_buf,
    k_mark,
    v_buf,
    pages_at,
    scores,
    weights,
    part,
    stat,
    part_in,
    stat_in,
    weigh,
    small_sem,
    k_sem,
    v_sem,
    q_send,
    q_recv,
    part_send,
    part_recv,
    stat_send,
    stat_recv,
):
    me = lax.axis_index("ctx")
    kvh, own, _ = q_ref.shape
    rows = new_k_ref.shape[1]
    cached = cache_k_ref.shape[0]
    pages = cached // PAGE
    total_rows = count * own
    block = min(BLOCK, total_rows)
    scale = HD ** (-0.5) * math.log2(math.e)

    def cache_copy(source, target, sems, k):
        return pltpu.make_async_copy(
            source.at[:, pl.ds(k * HD, HD)], target.at[k, pl.ds(0, cached)], sems.at[k]
        )

    barrier = pltpu.get_barrier_semaphore()
    for off in range(1, count):
        pl.semaphore_signal(
            barrier,
            inc=1,
            device_id={"ctx": lax.rem(me + off, count)},
            device_id_type=pl.DeviceIdType.MESH,
        )
    small = [
        pltpu.make_async_copy(source, target, small_sem.at[i])
        for i, (source, target) in enumerate(
            (
                (new_k_ref, new_k),
                (new_v_ref, new_v),
                (length_ref, length_at),
                (table_ref, table),
            )
        )
    ]
    own_q = pltpu.make_async_copy(q_ref, q_all.at[:, me], small_sem.at[len(small)])
    for copy in small:
        copy.start()
    own_q.start()
    for k in range(kvh):
        cache_copy(cache_k_ref, k_buf, k_sem, k).start()
        cache_copy(cache_v_ref, v_buf, v_sem, k).start()
    pl.semaphore_wait(barrier, count - 1)

    def q_copy(k, off):
        return pltpu.make_async_remote_copy(
            src_ref=q_ref.at[k],
            dst_ref=q_all.at[k, me],
            send_sem=q_send.at[k, off - 1],
            recv_sem=q_recv.at[k, off - 1],
            device_id={"ctx": lax.rem(me + off, count)},
            device_id_type=pl.DeviceIdType.MESH,
        )

    def part_copy(k, off):
        target = lax.rem(me + off, count)
        return pltpu.make_async_remote_copy(
            src_ref=part.at[k, target],
            dst_ref=part_in.at[k, me],
            send_sem=part_send.at[k, off - 1],
            recv_sem=part_recv.at[k, off - 1],
            device_id={"ctx": target},
            device_id_type=pl.DeviceIdType.MESH,
        )

    def stat_copy(k, off):
        target = lax.rem(me + off, count)
        return pltpu.make_async_remote_copy(
            src_ref=stat.at[k, target],
            dst_ref=stat_in.at[k, me],
            send_sem=stat_send.at[k, off - 1],
            recv_sem=stat_recv.at[k, off - 1],
            device_id={"ctx": target},
            device_id_type=pl.DeviceIdType.MESH,
        )

    for k in range(kvh):
        for off in range(1, count):
            q_copy(k, off).start()

    for copy in small:
        copy.wait()
    tail[...] = jnp.zeros_like(tail)
    for k in range(kvh):
        tail[0:rows, :] = new_k[k].astype(jnp.float32)
        k_buf[k, cached:, :] = tail[...].astype(jnp.bfloat16)
        tail[0:rows, :] = new_v[k].astype(jnp.float32)
        v_buf[k, cached:, :] = tail[...].astype(jnp.bfloat16)

    mark = q_mark.shape[1]
    row = lax.broadcasted_iota(jnp.int32, (total_rows, mark), 0)
    column = lax.broadcasted_iota(jnp.int32, (total_rows, mark), 1)
    token = (row // own) * rows + row % rows
    chosen = (column == 0) | (column == token + 1)
    q_mark[...] = jnp.where(chosen, 1.0, 0.0).astype(jnp.bfloat16)

    length = length_at[0]
    slots = me * pages + lax.broadcasted_iota(jnp.int32, (pages, table.shape[1]), 0)
    order = lax.broadcasted_iota(jnp.int32, (pages, table.shape[1]), 1)
    logical = jnp.sum(jnp.where(table[...] == slots, order, 0), axis=1, keepdims=True)
    pages_at[...] = jnp.broadcast_to(logical * PAGE, pages_at.shape)
    row = lax.broadcasted_iota(jnp.int32, (PAGE, mark), 0)
    column = lax.broadcasted_iota(jnp.int32, (PAGE, mark), 1)
    for j in range(pages):
        dead = (pages_at[j : j + 1, :] + row >= length) & (column == 0)
        k_mark[j * PAGE : (j + 1) * PAGE, :] = jnp.where(dead, FLOOR, 0.0).astype(jnp.bfloat16)
    later = (column > 0) & (column <= me * rows + row)
    dead = ((row < rows) & later) | ((row >= rows) & (column == 0))
    k_mark[cached:, :] = jnp.where(dead, FLOOR, 0.0).astype(jnp.bfloat16)

    keys = cached + PAGE
    spans = [(at, min(BLOCK, keys - at)) for at in range(0, keys, BLOCK)]
    parts = block // own

    def attend(k, at):
        query = jnp.concatenate(
            [
                q_all[k, pl.ds(at * parts, parts)].reshape(block, HD),
                q_mark[pl.ds(at * block, block), :],
            ],
            axis=1,
        )
        top = None
        for start, size in spans:
            span = slice(start, start + size)
            score = lax.dot_general(
                query,
                jnp.concatenate([k_buf[k, span, :], k_mark[span, :]], axis=1),
                (((1,), (1,)), ((), ())),
                preferred_element_type=jnp.float32,
            )
            scores[:, span] = score
            for page in range(size // PAGE):
                tile = score[:, page * PAGE : (page + 1) * PAGE]
                top = tile if top is None else jnp.maximum(top, tile)
        top = jnp.max(top, axis=1, keepdims=True)
        for start, size in spans:
            span = slice(start, start + size)
            weights[:, span] = jnp.exp2((scores[:, span] - top) * scale).astype(jnp.bfloat16)
        mixed = jnp.dot(
            weights[...],
            jnp.concatenate([v_buf[k], jnp.ones((keys, HD), jnp.bfloat16)], axis=1),
            preferred_element_type=jnp.float32,
        )
        total = mixed[:, HD:]
        mixed = mixed[:, :HD] * (1.0 / total)
        level = top * scale + jnp.log(total) * math.log2(math.e)
        lanes = lax.broadcasted_iota(jnp.int32, (own, HD), 1)
        columns = jnp.zeros((own, HD), jnp.float32)
        for i in range(parts):
            piece = slice(i * own, (i + 1) * own)
            part[k, at * parts + i] = mixed[piece].astype(jnp.bfloat16)
            columns = jnp.where(lanes == i, level[piece], columns)
        turned = columns.T
        for i in range(parts):
            stat[k, at * parts + i] = turned[i : i + 1, :]

    own_q.wait()

    def one_head(k, carry):
        for off in range(1, count):
            q_copy(k, off).wait_recv()
        cache_copy(cache_k_ref, k_buf, k_sem, k).wait()
        cache_copy(cache_v_ref, v_buf, v_sem, k).wait()
        if total_rows == block:
            attend(k, 0)
        else:
            lax.fori_loop(0, total_rows // block, lambda at, c: (attend(k, at), c)[1], 0)
        for off in range(1, count):
            part_copy(k, off).start()
            stat_copy(k, off).start()
        part_in[k, me] = part[k, me]
        stat_in[k, me] = stat[k, me]
        return carry

    lax.fori_loop(0, kvh, one_head, 0)

    def combine(k, carry):
        for off in range(1, count):
            part_copy(k, off).wait_recv()
            stat_copy(k, off).wait_recv()
        levels = [stat_in[k, s] for s in range(count)]
        top = functools.reduce(jnp.maximum, levels)
        shares = [jnp.exp2(level - top) for level in levels]
        share = 1.0 / functools.reduce(jnp.add, shares)
        for s in range(count):
            weigh[s : s + 1, :] = shares[s] * share
        turned = weigh[...].T
        result = jnp.zeros((own, HD), jnp.float32)
        for s in range(count):
            result = result + part_in[k, s].astype(jnp.float32) * turned[:, s : s + 1]
        out_ref[k] = result.astype(out_ref.dtype)
        return carry

    weigh[...] = jnp.zeros_like(weigh)
    lax.fori_loop(0, kvh, combine, 0)

    for k in range(kvh):
        for off in range(1, count):
            q_copy(k, off).wait_send()
            part_copy(k, off).wait_send()
            stat_copy(k, off).wait_send()


def local(queries, new_keys, new_values, cache_keys, cache_values, cache_length, page_table):
    count = lax.axis_size("ctx")
    rows, width = queries.shape
    heads = width // HD
    cached = cache_keys.shape[0]
    kvh = cache_keys.shape[1] // HD
    group = heads // kvh
    own = rows * group
    block = min(BLOCK, count * own)
    pages = cached // PAGE
    mark = -(-(1 + count * rows) // HD) * HD
    vmem = pl.BlockSpec(memory_space=pltpu.VMEM)
    held = pl.BlockSpec(memory_space=pltpu.HBM)
    dma = pltpu.SemaphoreType.DMA
    out = pl.pallas_call(
        functools.partial(kernel, count),
        out_shape=pltpu.VMEM((kvh, own, HD), jnp.bfloat16),
        in_specs=[held] * 7,
        out_specs=vmem,
        scratch_shapes=[
            pltpu.VMEM((kvh, rows, HD), jnp.bfloat16),
            pltpu.VMEM((kvh, rows, HD), jnp.bfloat16),
            pltpu.SMEM((1,), jnp.int32),
            pltpu.VMEM((1, page_table.shape[0]), jnp.int32),
            pltpu.VMEM((PAGE, HD), jnp.float32),
            pltpu.VMEM((kvh, count, own, HD), jnp.bfloat16),
            pltpu.VMEM((count * own, mark), jnp.bfloat16),
            pltpu.VMEM((kvh, cached + PAGE, HD), jnp.bfloat16),
            pltpu.VMEM((cached + PAGE, mark), jnp.bfloat16),
            pltpu.VMEM((kvh, cached + PAGE, HD), jnp.bfloat16),
            pltpu.VMEM((pages, mark), jnp.int32),
            pltpu.VMEM((block, cached + PAGE), jnp.float32),
            pltpu.VMEM((block, cached + PAGE), jnp.bfloat16),
            pltpu.VMEM((kvh, count, own, HD), jnp.bfloat16),
            pltpu.VMEM((kvh, count, 1, own), jnp.float32),
            pltpu.VMEM((kvh, count, own, HD), jnp.bfloat16),
            pltpu.VMEM((kvh, count, 1, own), jnp.float32),
            pltpu.VMEM((HD, own), jnp.float32),
            dma((5,)),
            dma((kvh,)),
            dma((kvh,)),
            dma((kvh, count - 1)),
            dma((kvh, count - 1)),
            dma((kvh, count - 1)),
            dma((kvh, count - 1)),
            dma((kvh, count - 1)),
            dma((kvh, count - 1)),
        ],
        compiler_params=pltpu.CompilerParams(
            collective_id=0, has_side_effects=True, vmem_limit_bytes=60 * 1024 * 1024
        ),
        cost_estimate=pl.CostEstimate(
            flops=4 * count * rows * heads * cached * HD,
            bytes_accessed=4 * cached * kvh * HD,
            transcendentals=count * rows * heads * cached,
        ),
        name="paged_attention",
    )(
        queries.reshape(rows, heads, HD).transpose(1, 0, 2).reshape(kvh, own, HD),
        new_keys.reshape(rows, kvh, HD).transpose(1, 0, 2),
        new_values.reshape(rows, kvh, HD).transpose(1, 0, 2),
        cache_keys,
        cache_values,
        cache_length,
        page_table.reshape(1, -1),
    )
    return out.reshape(heads, rows, HD).transpose(1, 0, 2).reshape(rows, width)


def solution(mesh):
    in_specs = (
        P(("req", "ctx"), None),
        P(("req", "ctx"), None),
        P(("req", "ctx"), None),
        P(("req", "ctx"), None),
        P(("req", "ctx"), None),
        P("req"),
        P("req"),
    )
    out_specs = P(("req", "ctx"), None)
    return jax.shard_map(local, mesh=mesh, in_specs=in_specs, out_specs=out_specs, check_vma=False)
```

```python
import functools
import math

import jax
import jax.numpy as jnp
from jax import lax
from jax.experimental import pallas as pl
from jax.experimental.pallas import tpu as pltpu
from jax.sharding import PartitionSpec as P

HD = 128
PAGE = 128
FLOOR = -1e30
BLOCK = 256


def kernel(
    count,
    q_ref,
    new_k_ref,
    new_v_ref,
    cache_k_ref,
    cache_v_ref,
    length_ref,
    table_ref,
    out_ref,
    new_k,
    new_v,
    length_at,
    table,
    tail,
    q_all,
    k_buf,
    k_turned,
    v_buf,
    bias,
    scores,
    tops,
    part,
    stat,
    part_in,
    stat_in,
    weigh,
    small_sem,
    k_sem,
    v_sem,
    q_send,
    q_recv,
    part_send,
    part_recv,
    stat_send,
    stat_recv,
):
    me = lax.axis_index("ctx")
    kvh, own, _ = q_ref.shape
    rows = new_k_ref.shape[1]
    cached = cache_k_ref.shape[0]
    pages = cached // PAGE
    total_rows = count * own
    block = min(BLOCK, total_rows)
    scale = HD ** (-0.5) * math.log2(math.e)

    def cache_copy(source, target, sems, k):
        return pltpu.make_async_copy(
            source.at[:, pl.ds(k * HD, HD)], target.at[k, pl.ds(0, cached)], sems.at[k]
        )

    barrier = pltpu.get_barrier_semaphore()
    for off in range(1, count):
        pl.semaphore_signal(
            barrier,
            inc=1,
            device_id={"ctx": lax.rem(me + off, count)},
            device_id_type=pl.DeviceIdType.MESH,
        )
    small = [
        pltpu.make_async_copy(source, target, small_sem.at[i])
        for i, (source, target) in enumerate(
            (
                (new_k_ref, new_k),
                (new_v_ref, new_v),
                (length_ref, length_at),
                (table_ref, table),
            )
        )
    ]
    own_q = pltpu.make_async_copy(q_ref, q_all.at[:, me], small_sem.at[len(small)])
    for copy in small:
        copy.start()
    own_q.start()
    for k in range(kvh):
        cache_copy(cache_k_ref, k_buf, k_sem, k).start()
    for k in range(kvh):
        cache_copy(cache_v_ref, v_buf, v_sem, k).start()
    pl.semaphore_wait(barrier, count - 1)

    def q_copy(k, off):
        return pltpu.make_async_remote_copy(
            src_ref=q_ref.at[k],
            dst_ref=q_all.at[k, me],
            send_sem=q_send.at[k, off - 1],
            recv_sem=q_recv.at[k, off - 1],
            device_id={"ctx": lax.rem(me + off, count)},
            device_id_type=pl.DeviceIdType.MESH,
        )

    def part_copy(k, off):
        target = lax.rem(me + off, count)
        return pltpu.make_async_remote_copy(
            src_ref=part.at[k, target],
            dst_ref=part_in.at[k, me],
            send_sem=part_send.at[k, off - 1],
            recv_sem=part_recv.at[k, off - 1],
            device_id={"ctx": target},
            device_id_type=pl.DeviceIdType.MESH,
        )

    def stat_copy(k, off):
        target = lax.rem(me + off, count)
        return pltpu.make_async_remote_copy(
            src_ref=stat.at[k, target],
            dst_ref=stat_in.at[k, me],
            send_sem=stat_send.at[k, off - 1],
            recv_sem=stat_recv.at[k, off - 1],
            device_id={"ctx": target},
            device_id_type=pl.DeviceIdType.MESH,
        )

    for k in range(kvh):
        for off in range(1, count):
            q_copy(k, off).start()

    for copy in small:
        copy.wait()
    tail[...] = jnp.zeros_like(tail)
    for k in range(kvh):
        tail[0:rows, :] = new_k[k].astype(jnp.float32)
        k_buf[k, cached:, :] = tail[...].astype(jnp.bfloat16)
        tail[0:rows, :] = new_v[k].astype(jnp.float32)
        v_buf[k, cached:, :] = tail[...].astype(jnp.bfloat16)

    length = length_at[0]
    slots = me * pages + lax.broadcasted_iota(jnp.int32, (pages, table.shape[1]), 0)
    order = lax.broadcasted_iota(jnp.int32, (pages, table.shape[1]), 1)
    hits = jnp.where(table[...] == slots, order, 0)
    logical = jnp.sum(hits, axis=1, keepdims=True)
    lane = lax.broadcasted_iota(jnp.int32, (pages, PAGE), 1)
    bias[...] = jnp.where(logical * PAGE + lane < length, 0.0, FLOOR)

    keys = cached + PAGE
    spans = [(start, min(BLOCK, keys - start)) for start in range(0, keys, BLOCK)]
    parts = block // own

    for k in range(kvh):
        cache_copy(cache_k_ref, k_buf, k_sem, k).wait()
        k_turned[k] = k_buf[k].T

    def mask_new(score, at):
        row = at * block + lax.broadcasted_iota(jnp.int32, (block, PAGE), 0)
        column = lax.broadcasted_iota(jnp.int32, (block, PAGE), 1)
        token = (row // own) * rows + row % rows
        allowed = (column < rows) & (me * rows + column <= token)
        return jnp.where(allowed, score * scale, FLOOR)

    def step(ahead, now, at):
        held = pl.ds(at * block, block)
        if ahead is not None:
            query = q_all[ahead, pl.ds(at * parts, parts)].reshape(block, HD)
            slot = lax.rem(ahead, 2)
            top = None
        if now is not None:
            slot_now = lax.rem(now, 2)
            top_now = tops[slot_now, held, :]
            summed = jnp.zeros((block, PAGE), jnp.float32)
            mixed = jnp.zeros((block, HD), jnp.float32)
        for start, size in spans:
            if ahead is not None:
                score = jnp.dot(
                    query,
                    k_turned[ahead, :, start : start + size],
                    preferred_element_type=jnp.float32,
                )
                for page in range(size // PAGE):
                    j = start // PAGE + page
                    tile = score[:, page * PAGE : (page + 1) * PAGE]
                    if j < pages:
                        tile = tile * scale + bias[j : j + 1, :]
                    else:
                        tile = mask_new(tile, at)
                    scores[slot, held, j * PAGE : (j + 1) * PAGE] = tile
                    top = tile if top is None else jnp.maximum(top, tile)
            if now is not None:
                weights = []
                for at_key in range(start, start + size, PAGE):
                    weight = jnp.exp2(scores[slot_now, held, at_key : at_key + PAGE] - top_now)
                    summed = summed + weight
                    weights.append(weight.astype(jnp.bfloat16))
                mixed = mixed + jnp.dot(
                    jnp.concatenate(weights, axis=1),
                    v_buf[now, start : start + size, :],
                    preferred_element_type=jnp.float32,
                )
        if ahead is not None:
            top = jnp.max(top, axis=1, keepdims=True)
            tops[slot, held, :] = jnp.broadcast_to(top, (block, PAGE))
        if now is not None:
            total = jnp.sum(summed, axis=1, keepdims=True)
            mixed = mixed * (1.0 / total)
            level = top_now + jnp.log(total) * math.log2(math.e)
            lanes = lax.broadcasted_iota(jnp.int32, (own, HD), 1)
            columns = jnp.zeros((own, HD), jnp.float32)
            for i in range(parts):
                piece = slice(i * own, (i + 1) * own)
                part[now, at * parts + i] = mixed[piece].astype(jnp.bfloat16)
                columns = jnp.where(lanes == i, level[piece], columns)
            turned = columns.T
            for i in range(parts):
                stat[now, at * parts + i] = turned[i : i + 1, :]

    def run(ahead, now):
        if ahead is not None:
            for off in range(1, count):
                q_copy(ahead, off).wait_recv()
        if now is not None:
            cache_copy(cache_v_ref, v_buf, v_sem, now).wait()
        if total_rows == block:
            step(ahead, now, 0)
        else:
            lax.fori_loop(0, total_rows // block, lambda at, c: (step(ahead, now, at), c)[1], 0)
        if now is not None:
            for off in range(1, count):
                part_copy(now, off).start()
                stat_copy(now, off).start()
            part_in[now, me] = part[now, me]
            stat_in[now, me] = stat[now, me]

    own_q.wait()
    run(0, None)
    lax.fori_loop(0, kvh - 1, lambda k, c: (run(k + 1, k), c)[1], 0)
    run(None, kvh - 1)

    def combine(k, carry):
        for off in range(1, count):
            part_copy(k, off).wait_recv()
            stat_copy(k, off).wait_recv()
        levels = [stat_in[k, s] for s in range(count)]
        top = functools.reduce(jnp.maximum, levels)
        shares = [jnp.exp2(level - top) for level in levels]
        share = 1.0 / functools.reduce(jnp.add, shares)
        for s in range(count):
            weigh[s : s + 1, :] = shares[s] * share
        turned = weigh[...].T
        result = jnp.zeros((own, HD), jnp.float32)
        for s in range(count):
            result = result + part_in[k, s].astype(jnp.float32) * turned[:, s : s + 1]
        out_ref[k] = result.astype(out_ref.dtype)
        return carry

    weigh[...] = jnp.zeros_like(weigh)
    lax.fori_loop(0, kvh - 1, combine, 0)
    for k in range(kvh):
        for off in range(1, count):
            q_copy(k, off).wait_send()
            part_copy(k, off).wait_send()
            stat_copy(k, off).wait_send()
    combine(kvh - 1, 0)


def local(queries, new_keys, new_values, cache_keys, cache_values, cache_length, page_table):
    count = lax.axis_size("ctx")
    rows, width = queries.shape
    heads = width // HD
    cached = cache_keys.shape[0]
    kvh = cache_keys.shape[1] // HD
    group = heads // kvh
    own = rows * group
    block = min(BLOCK, count * own)
    pages = cached // PAGE
    vmem = pl.BlockSpec(memory_space=pltpu.VMEM)
    held = pl.BlockSpec(memory_space=pltpu.HBM)
    dma = pltpu.SemaphoreType.DMA
    out = pl.pallas_call(
        functools.partial(kernel, count),
        out_shape=pltpu.VMEM((kvh, own, HD), jnp.bfloat16),
        in_specs=[held] * 7,
        out_specs=vmem,
        scratch_shapes=[
            pltpu.VMEM((kvh, rows, HD), jnp.bfloat16),
            pltpu.VMEM((kvh, rows, HD), jnp.bfloat16),
            pltpu.SMEM((1,), jnp.int32),
            pltpu.VMEM((1, page_table.shape[0]), jnp.int32),
            pltpu.VMEM((PAGE, HD), jnp.float32),
            pltpu.VMEM((kvh, count, own, HD), jnp.bfloat16),
            pltpu.VMEM((kvh, cached + PAGE, HD), jnp.bfloat16),
            pltpu.VMEM((kvh, HD, cached + PAGE), jnp.bfloat16),
            pltpu.VMEM((kvh, cached + PAGE, HD), jnp.bfloat16),
            pltpu.VMEM((pages, PAGE), jnp.float32),
            pltpu.VMEM((2, count * own, cached + PAGE), jnp.float32),
            pltpu.VMEM((2, count * own, PAGE), jnp.float32),
            pltpu.VMEM((kvh, count, own, HD), jnp.bfloat16),
            pltpu.VMEM((kvh, count, 1, own), jnp.float32),
            pltpu.VMEM((kvh, count, own, HD), jnp.bfloat16),
            pltpu.VMEM((kvh, count, 1, own), jnp.float32),
            pltpu.VMEM((HD, own), jnp.float32),
            dma((5,)),
            dma((kvh,)),
            dma((kvh,)),
            dma((kvh, count - 1)),
            dma((kvh, count - 1)),
            dma((kvh, count - 1)),
            dma((kvh, count - 1)),
            dma((kvh, count - 1)),
            dma((kvh, count - 1)),
        ],
        compiler_params=pltpu.CompilerParams(
            collective_id=0, has_side_effects=True, vmem_limit_bytes=60 * 1024 * 1024
        ),
        cost_estimate=pl.CostEstimate(
            flops=4 * count * rows * heads * cached * HD,
            bytes_accessed=4 * cached * kvh * HD,
            transcendentals=count * rows * heads * cached,
        ),
        name="paged_attention",
    )(
        queries.reshape(rows, heads, HD).transpose(1, 0, 2).reshape(kvh, own, HD),
        new_keys.reshape(rows, kvh, HD).transpose(1, 0, 2),
        new_values.reshape(rows, kvh, HD).transpose(1, 0, 2),
        cache_keys,
        cache_values,
        cache_length,
        page_table.reshape(1, -1),
    )
    return out.reshape(heads, rows, HD).transpose(1, 0, 2).reshape(rows, width)


def solution(mesh):
    in_specs = (
        P(("req", "ctx"), None),
        P(("req", "ctx"), None),
        P(("req", "ctx"), None),
        P(("req", "ctx"), None),
        P(("req", "ctx"), None),
        P("req"),
        P("req"),
    )
    out_specs = P(("req", "ctx"), None)
    return jax.shard_map(local, mesh=mesh, in_specs=in_specs, out_specs=out_specs, check_vma=False)
```

```python
import functools
import math

import jax
import jax.numpy as jnp
from jax import lax
from jax.experimental import pallas as pl
from jax.experimental.pallas import tpu as pltpu
from jax.sharding import PartitionSpec as P

HD = 128
PAGE = 128
FLOOR = -1e30
BLOCK = 256


def kernel(
    count,
    q_ref,
    new_k_ref,
    new_v_ref,
    cache_k_ref,
    cache_v_ref,
    length_ref,
    table_ref,
    out_ref,
    new_k,
    new_v,
    length_at,
    table,
    tail,
    q_all,
    k_buf,
    v_buf,
    bias,
    scores,
    part,
    stat,
    part_in,
    stat_in,
    weigh,
    small_sem,
    k_sem,
    v_sem,
    q_send,
    q_recv,
    part_send,
    part_recv,
    stat_send,
    stat_recv,
):
    me = lax.axis_index("ctx")
    kvh, own, _ = q_ref.shape
    rows = new_k_ref.shape[1]
    cached = cache_k_ref.shape[0]
    pages = cached // PAGE
    total_rows = count * own
    block = min(BLOCK, total_rows)
    scale = HD ** (-0.5) * math.log2(math.e)

    def cache_copy(source, target, sems, k):
        return pltpu.make_async_copy(
            source.at[:, pl.ds(k * HD, HD)], target.at[k, pl.ds(0, cached)], sems.at[k]
        )

    barrier = pltpu.get_barrier_semaphore()
    for off in range(1, count):
        pl.semaphore_signal(
            barrier,
            inc=1,
            device_id={"ctx": lax.rem(me + off, count)},
            device_id_type=pl.DeviceIdType.MESH,
        )
    small = [
        pltpu.make_async_copy(source, target, small_sem.at[i])
        for i, (source, target) in enumerate(
            (
                (new_k_ref, new_k),
                (new_v_ref, new_v),
                (length_ref, length_at),
                (table_ref, table),
            )
        )
    ]
    own_q = pltpu.make_async_copy(q_ref, q_all.at[:, me], small_sem.at[len(small)])
    for copy in small:
        copy.start()
    own_q.start()
    cache_copy(cache_k_ref, k_buf, k_sem, 0).start()
    cache_copy(cache_v_ref, v_buf, v_sem, 0).start()
    pl.semaphore_wait(barrier, count - 1)

    def q_copy(k, off):
        return pltpu.make_async_remote_copy(
            src_ref=q_ref.at[k],
            dst_ref=q_all.at[k, me],
            send_sem=q_send.at[k, off - 1],
            recv_sem=q_recv.at[k, off - 1],
            device_id={"ctx": lax.rem(me + off, count)},
            device_id_type=pl.DeviceIdType.MESH,
        )

    def part_copy(k, off):
        target = lax.rem(me + off, count)
        return pltpu.make_async_remote_copy(
            src_ref=part.at[k, target],
            dst_ref=part_in.at[k, me],
            send_sem=part_send.at[k, off - 1],
            recv_sem=part_recv.at[k, off - 1],
            device_id={"ctx": target},
            device_id_type=pl.DeviceIdType.MESH,
        )

    def stat_copy(k, off):
        target = lax.rem(me + off, count)
        return pltpu.make_async_remote_copy(
            src_ref=stat.at[k, target],
            dst_ref=stat_in.at[k, me],
            send_sem=stat_send.at[k, off - 1],
            recv_sem=stat_recv.at[k, off - 1],
            device_id={"ctx": target},
            device_id_type=pl.DeviceIdType.MESH,
        )

    for k in range(kvh):
        for off in range(1, count):
            q_copy(k, off).start()
    for k in range(1, kvh):
        cache_copy(cache_k_ref, k_buf, k_sem, k).start()
        cache_copy(cache_v_ref, v_buf, v_sem, k).start()

    for copy in small:
        copy.wait()
    tail[...] = jnp.zeros_like(tail)
    for k in range(kvh):
        tail[0:rows, :] = new_k[k].astype(jnp.float32)
        k_buf[k, cached:, :] = tail[...].astype(jnp.bfloat16)
        tail[0:rows, :] = new_v[k].astype(jnp.float32)
        v_buf[k, cached:, :] = tail[...].astype(jnp.bfloat16)

    length = length_at[0]
    slots = me * pages + lax.broadcasted_iota(jnp.int32, (pages, table.shape[1]), 0)
    order = lax.broadcasted_iota(jnp.int32, (pages, table.shape[1]), 1)
    hits = jnp.where(table[...] == slots, order, 0)
    logical = jnp.sum(hits, axis=1, keepdims=True)
    lane = lax.broadcasted_iota(jnp.int32, (pages, PAGE), 1)
    bias[...] = jnp.where(logical * PAGE + lane < length, 0.0, FLOOR)

    spans = [(at, min(BLOCK, cached - at)) for at in range(0, cached, BLOCK)]

    def attend(k, at):
        if total_rows == block:
            query = q_all[k].reshape(total_rows, HD)
        else:
            parts = block // own
            query = q_all[k, pl.ds(at * parts, parts)].reshape(block, HD)
        top = None
        for start, size in spans:
            score = lax.dot_general(
                query,
                k_buf[k, start : start + size, :],
                (((1,), (1,)), ((), ())),
                preferred_element_type=jnp.float32,
            )
            for page in range(size // PAGE):
                j = start // PAGE + page
                tile = score[:, page * PAGE : (page + 1) * PAGE] * scale + bias[j : j + 1, :]
                scores[:, j * PAGE : (j + 1) * PAGE] = tile
                top = tile if top is None else jnp.maximum(top, tile)
        score = lax.dot_general(
            query,
            k_buf[k, cached:, :],
            (((1,), (1,)), ((), ())),
            preferred_element_type=jnp.float32,
        )
        row = at * block + lax.broadcasted_iota(jnp.int32, (block, PAGE), 0)
        column = lax.broadcasted_iota(jnp.int32, (block, PAGE), 1)
        token = (row // own) * rows + row % rows
        allowed = (column < rows) & (me * rows + column <= token)
        last = jnp.where(allowed, score * scale, FLOOR)
        top = jnp.max(jnp.maximum(top, last), axis=1, keepdims=True)
        weight = jnp.exp2(last - top)
        summed = weight
        mixed = jnp.dot(
            weight.astype(jnp.bfloat16), v_buf[k, cached:, :], preferred_element_type=jnp.float32
        )
        for start, size in spans:
            weight = jnp.exp2(scores[:, start : start + size] - top)
            for page in range(size // PAGE):
                summed = summed + weight[:, page * PAGE : (page + 1) * PAGE]
            mixed = mixed + jnp.dot(
                weight.astype(jnp.bfloat16),
                v_buf[k, start : start + size, :],
                preferred_element_type=jnp.float32,
            )
        total = jnp.sum(summed, axis=1, keepdims=True)
        mixed = mixed * (1.0 / total)
        level = top + jnp.log(total) * math.log2(math.e)
        lanes = lax.broadcasted_iota(jnp.int32, (own, HD), 1)
        columns = jnp.zeros((own, HD), jnp.float32)
        for i in range(block // own):
            piece = slice(i * own, (i + 1) * own)
            part[k, at * (block // own) + i] = mixed[piece].astype(jnp.bfloat16)
            columns = jnp.where(lanes == i, level[piece], columns)
        turned = columns.T
        for i in range(block // own):
            stat[k, at * (block // own) + i] = turned[i : i + 1, :]

    own_q.wait()

    def one_head(k, carry):
        for off in range(1, count):
            q_copy(k, off).wait_recv()
        cache_copy(cache_k_ref, k_buf, k_sem, k).wait()
        cache_copy(cache_v_ref, v_buf, v_sem, k).wait()
        if total_rows == block:
            attend(k, 0)
        else:
            lax.fori_loop(0, total_rows // block, lambda at, c: (attend(k, at), c)[1], 0)
        for off in range(1, count):
            part_copy(k, off).start()
            stat_copy(k, off).start()
        part_in[k, me] = part[k, me]
        stat_in[k, me] = stat[k, me]
        return carry

    lax.fori_loop(0, kvh, one_head, 0)

    def combine(k, carry):
        for off in range(1, count):
            part_copy(k, off).wait_recv()
            stat_copy(k, off).wait_recv()
        levels = [stat_in[k, s] for s in range(count)]
        top = functools.reduce(jnp.maximum, levels)
        shares = [jnp.exp2(level - top) for level in levels]
        share = 1.0 / functools.reduce(jnp.add, shares)
        for s in range(count):
            weigh[s : s + 1, :] = shares[s] * share
        turned = weigh[...].T
        result = jnp.zeros((own, HD), jnp.float32)
        for s in range(count):
            result = result + part_in[k, s].astype(jnp.float32) * turned[:, s : s + 1]
        out_ref[k] = result.astype(out_ref.dtype)
        return carry

    weigh[...] = jnp.zeros_like(weigh)
    lax.fori_loop(0, kvh - 1, combine, 0)
    for k in range(kvh):
        for off in range(1, count):
            q_copy(k, off).wait_send()
            part_copy(k, off).wait_send()
            stat_copy(k, off).wait_send()
    combine(kvh - 1, 0)


def local(queries, new_keys, new_values, cache_keys, cache_values, cache_length, page_table):
    count = lax.axis_size("ctx")
    rows, width = queries.shape
    heads = width // HD
    cached = cache_keys.shape[0]
    kvh = cache_keys.shape[1] // HD
    group = heads // kvh
    own = rows * group
    block = min(BLOCK, count * own)
    pages = cached // PAGE
    vmem = pl.BlockSpec(memory_space=pltpu.VMEM)
    held = pl.BlockSpec(memory_space=pltpu.HBM)
    dma = pltpu.SemaphoreType.DMA
    out = pl.pallas_call(
        functools.partial(kernel, count),
        out_shape=pltpu.VMEM((kvh, own, HD), jnp.bfloat16),
        in_specs=[held] * 7,
        out_specs=vmem,
        scratch_shapes=[
            pltpu.VMEM((kvh, rows, HD), jnp.bfloat16),
            pltpu.VMEM((kvh, rows, HD), jnp.bfloat16),
            pltpu.SMEM((1,), jnp.int32),
            pltpu.VMEM((1, page_table.shape[0]), jnp.int32),
            pltpu.VMEM((PAGE, HD), jnp.float32),
            pltpu.VMEM((kvh, count, own, HD), jnp.bfloat16),
            pltpu.VMEM((kvh, cached + PAGE, HD), jnp.bfloat16),
            pltpu.VMEM((kvh, cached + PAGE, HD), jnp.bfloat16),
            pltpu.VMEM((pages, PAGE), jnp.float32),
            pltpu.VMEM((block, cached), jnp.float32),
            pltpu.VMEM((kvh, count, own, HD), jnp.bfloat16),
            pltpu.VMEM((kvh, count, 1, own), jnp.float32),
            pltpu.VMEM((kvh, count, own, HD), jnp.bfloat16),
            pltpu.VMEM((kvh, count, 1, own), jnp.float32),
            pltpu.VMEM((HD, own), jnp.float32),
            dma((5,)),
            dma((kvh,)),
            dma((kvh,)),
            dma((kvh, count - 1)),
            dma((kvh, count - 1)),
            dma((kvh, count - 1)),
            dma((kvh, count - 1)),
            dma((kvh, count - 1)),
            dma((kvh, count - 1)),
        ],
        compiler_params=pltpu.CompilerParams(
            collective_id=0, has_side_effects=True, vmem_limit_bytes=60 * 1024 * 1024
        ),
        cost_estimate=pl.CostEstimate(
            flops=4 * count * rows * heads * cached * HD,
            bytes_accessed=4 * cached * kvh * HD,
            transcendentals=count * rows * heads * cached,
        ),
        name="paged_attention",
    )(
        queries.reshape(rows, heads, HD).transpose(1, 0, 2).reshape(kvh, own, HD),
        new_keys.reshape(rows, kvh, HD).transpose(1, 0, 2),
        new_values.reshape(rows, kvh, HD).transpose(1, 0, 2),
        cache_keys,
        cache_values,
        cache_length,
        page_table.reshape(1, -1),
    )
    return out.reshape(heads, rows, HD).transpose(1, 0, 2).reshape(rows, width)


def solution(mesh):
    in_specs = (
        P(("req", "ctx"), None),
        P(("req", "ctx"), None),
        P(("req", "ctx"), None),
        P(("req", "ctx"), None),
        P(("req", "ctx"), None),
        P("req"),
        P("req"),
    )
    out_specs = P(("req", "ctx"), None)
    return jax.shard_map(local, mesh=mesh, in_specs=in_specs, out_specs=out_specs, check_vma=False)
```

```python
import functools
import math

import jax
import jax.numpy as jnp
from jax import lax
from jax.experimental import pallas as pl
from jax.experimental.pallas import tpu as pltpu
from jax.sharding import PartitionSpec as P

HD = 128
PAGE = 128
FLOOR = -1e30
BLOCK = 256
ROWS = 128


def kernel(
    count,
    q_ref,
    new_k_ref,
    new_v_ref,
    cache_k_ref,
    cache_v_ref,
    length_ref,
    table_ref,
    out_ref,
    new_k,
    new_v,
    length_at,
    table,
    tail,
    q_all,
    k_buf,
    v_buf,
    bias,
    bias_new,
    scores,
    part,
    stat,
    part_in,
    stat_in,
    weigh,
    small_sem,
    k_sem,
    v_sem,
    q_send,
    q_recv,
    part_send,
    part_recv,
    stat_send,
    stat_recv,
):
    me = lax.axis_index("ctx")
    kvh, own, _ = q_ref.shape
    rows = new_k_ref.shape[1]
    cached = cache_k_ref.shape[0]
    pages = cached // PAGE
    total_rows = count * own
    block = min(ROWS, total_rows)
    scale = HD ** (-0.5) * math.log2(math.e)

    def each_head(body):
        lax.fori_loop(0, kvh, lambda k, carry: (body(k), carry)[1], 0)

    def cache_copy(source, target, sems, k):
        return pltpu.make_async_copy(
            source.at[:, pl.ds(pl.multiple_of(k * HD, HD), HD)], target.at[k, pl.ds(0, cached)], sems.at[k]
        )

    barrier = pltpu.get_barrier_semaphore()
    for off in range(1, count):
        pl.semaphore_signal(
            barrier,
            inc=1,
            device_id={"ctx": lax.rem(me + off, count)},
            device_id_type=pl.DeviceIdType.MESH,
        )
    small = [
        pltpu.make_async_copy(source, target, small_sem.at[i])
        for i, (source, target) in enumerate(
            (
                (new_k_ref, new_k),
                (new_v_ref, new_v),
                (length_ref, length_at),
                (table_ref, table),
            )
        )
    ]
    own_q = pltpu.make_async_copy(q_ref, q_all.at[:, me], small_sem.at[len(small)])
    for copy in small:
        copy.start()
    own_q.start()
    cache_copy(cache_k_ref, k_buf, k_sem, 0).start()
    cache_copy(cache_v_ref, v_buf, v_sem, 0).start()
    pl.semaphore_wait(barrier, count - 1)

    def q_copy(k, off):
        return pltpu.make_async_remote_copy(
            src_ref=q_ref.at[k],
            dst_ref=q_all.at[k, me],
            send_sem=q_send.at[k, off - 1],
            recv_sem=q_recv.at[k, off - 1],
            device_id={"ctx": lax.rem(me + off, count)},
            device_id_type=pl.DeviceIdType.MESH,
        )

    def part_copy(k, off):
        target = lax.rem(me + off, count)
        return pltpu.make_async_remote_copy(
            src_ref=part.at[k, target],
            dst_ref=part_in.at[k, me],
            send_sem=part_send.at[k, off - 1],
            recv_sem=part_recv.at[k, off - 1],
            device_id={"ctx": target},
            device_id_type=pl.DeviceIdType.MESH,
        )

    def stat_copy(k, off):
        target = lax.rem(me + off, count)
        return pltpu.make_async_remote_copy(
            src_ref=stat.at[k, target],
            dst_ref=stat_in.at[k, me],
            send_sem=stat_send.at[k, off - 1],
            recv_sem=stat_recv.at[k, off - 1],
            device_id={"ctx": target},
            device_id_type=pl.DeviceIdType.MESH,
        )

    @each_head
    def _(k):
        for off in range(1, count):
            q_copy(k, off).start()

    @functools.partial(lax.fori_loop, 1, kvh, init_val=0)
    def _(k, carry):
        cache_copy(cache_k_ref, k_buf, k_sem, k).start()
        cache_copy(cache_v_ref, v_buf, v_sem, k).start()
        return carry


    for copy in small:
        copy.wait()
    tail[...] = jnp.zeros_like(tail)
    @each_head
    def _(k):
        tail[0:rows, :] = new_k[k].astype(jnp.float32)
        k_buf[k, cached:, :] = tail[...].astype(jnp.bfloat16)
        tail[0:rows, :] = new_v[k].astype(jnp.float32)
        v_buf[k, cached:, :] = tail[...].astype(jnp.bfloat16)

    length = length_at[0]
    slots = me * pages + lax.broadcasted_iota(jnp.int32, (pages, table.shape[1]), 0)
    order = lax.broadcasted_iota(jnp.int32, (pages, table.shape[1]), 1)
    hits = jnp.where(table[...] == slots, order, 0)
    logical = jnp.sum(hits, axis=1, keepdims=True)
    lane = lax.broadcasted_iota(jnp.int32, (pages, PAGE), 1)
    bias[...] = jnp.where(logical * PAGE + lane < length, 0.0, FLOOR)

    token = lax.rem(lax.broadcasted_iota(jnp.int32, (own, PAGE), 0), rows)
    column = lax.broadcasted_iota(jnp.int32, (own, PAGE), 1)
    first = jnp.where(column < rows, me * rows + column - token, count * rows)
    for s in range(count):
        bias_new[s] = jnp.where(first <= s * rows, 0.0, FLOOR)

    spans = [(at, min(BLOCK, cached - at)) for at in range(0, cached, BLOCK)]

    def attend(k, at):
        if total_rows == block:
            query = q_all[k].reshape(total_rows, HD)
        else:
            parts = block // own
            query = q_all[k, pl.ds(at * parts, parts)].reshape(block, HD)
        top = None
        for start, size in spans:
            score = lax.dot_general(
                query,
                k_buf[k, start : start + size, :],
                (((1,), (1,)), ((), ())),
                preferred_element_type=jnp.float32,
            )
            for page in range(size // PAGE):
                j = start // PAGE + page
                tile = score[:, page * PAGE : (page + 1) * PAGE] * scale + bias[j : j + 1, :]
                scores[:, j * PAGE : (j + 1) * PAGE] = tile
                top = tile if top is None else jnp.maximum(top, tile)
        score = lax.dot_general(
            query,
            k_buf[k, cached:, :],
            (((1,), (1,)), ((), ())),
            preferred_element_type=jnp.float32,
        )
        barred = bias_new[pl.ds(at * (block // own), block // own)].reshape(block, PAGE)
        last = score * scale + barred
        top = jnp.max(jnp.maximum(top, last), axis=1, keepdims=True)
        weight = jnp.exp2(last - top)
        summed = weight
        mixed = jnp.dot(
            weight.astype(jnp.bfloat16), v_buf[k, cached:, :], preferred_element_type=jnp.float32
        )
        for start, size in spans:
            weight = jnp.exp2(scores[:, start : start + size] - top)
            for page in range(size // PAGE):
                summed = summed + weight[:, page * PAGE : (page + 1) * PAGE]
            mixed = mixed + jnp.dot(
                weight.astype(jnp.bfloat16),
                v_buf[k, start : start + size, :],
                preferred_element_type=jnp.float32,
            )
        total = jnp.sum(summed, axis=1, keepdims=True)
        mixed = mixed * (1.0 / total)
        level = top + jnp.log(total) * math.log2(math.e)
        lanes = lax.broadcasted_iota(jnp.int32, (own, HD), 1)
        columns = jnp.zeros((own, HD), jnp.float32)
        for i in range(block // own):
            piece = slice(i * own, (i + 1) * own)
            part[k, at * (block // own) + i] = mixed[piece].astype(jnp.bfloat16)
            columns = jnp.where(lanes == i, level[piece], columns)
        turned = columns.T
        for i in range(block // own):
            stat[k, at * (block // own) + i] = turned[i : i + 1, :]

    own_q.wait()

    def one_head(k, carry):
        for off in range(1, count):
            q_copy(k, off).wait_recv()
        cache_copy(cache_k_ref, k_buf, k_sem, k).wait()
        cache_copy(cache_v_ref, v_buf, v_sem, k).wait()
        if total_rows == block:
            attend(k, 0)
        else:
            lax.fori_loop(0, total_rows // block, lambda at, c: (attend(k, at), c)[1], 0)
        for off in range(1, count):
            part_copy(k, off).start()
            stat_copy(k, off).start()
        part_in[k, me] = part[k, me]
        stat_in[k, me] = stat[k, me]
        return carry

    lax.fori_loop(0, kvh, one_head, 0)

    def combine(k, carry):
        for off in range(1, count):
            part_copy(k, off).wait_recv()
            stat_copy(k, off).wait_recv()
        for off in range(1, count):
            q_copy(k, off).wait_send()
            part_copy(k, off).wait_send()
            stat_copy(k, off).wait_send()
        levels = [stat_in[k, s] for s in range(count)]
        top = functools.reduce(jnp.maximum, levels)
        shares = [jnp.exp2(level - top) for level in levels]
        share = 1.0 / functools.reduce(jnp.add, shares)
        for s in range(count):
            weigh[s : s + 1, :] = shares[s] * share
        turned = weigh[...].T
        result = jnp.zeros((own, HD), jnp.float32)
        for s in range(count):
            result = result + part_in[k, s].astype(jnp.float32) * turned[:, s : s + 1]
        out_ref[k] = result.astype(out_ref.dtype)
        return carry

    weigh[...] = jnp.zeros_like(weigh)
    lax.fori_loop(0, kvh, combine, 0)


def local(queries, new_keys, new_values, cache_keys, cache_values, cache_length, page_table):
    count = lax.axis_size("ctx")
    rows, width = queries.shape
    heads = width // HD
    cached = cache_keys.shape[0]
    kvh = cache_keys.shape[1] // HD
    group = heads // kvh
    own = rows * group
    block = min(ROWS, count * own)
    pages = cached // PAGE
    vmem = pl.BlockSpec(memory_space=pltpu.VMEM)
    held = pl.BlockSpec(memory_space=pltpu.HBM)
    dma = pltpu.SemaphoreType.DMA
    out = pl.pallas_call(
        functools.partial(kernel, count),
        out_shape=pltpu.VMEM((kvh, own, HD), jnp.bfloat16),
        in_specs=[held] * 7,
        out_specs=vmem,
        scratch_shapes=[
            pltpu.VMEM((kvh, rows, HD), jnp.bfloat16),
            pltpu.VMEM((kvh, rows, HD), jnp.bfloat16),
            pltpu.SMEM((1,), jnp.int32),
            pltpu.VMEM((1, page_table.shape[0]), jnp.int32),
            pltpu.VMEM((PAGE, HD), jnp.float32),
            pltpu.VMEM((kvh, count, own, HD), jnp.bfloat16),
            pltpu.VMEM((kvh, cached + PAGE, HD), jnp.bfloat16),
            pltpu.VMEM((kvh, cached + PAGE, HD), jnp.bfloat16),
            pltpu.VMEM((pages, PAGE), jnp.float32),
            pltpu.VMEM((count, own, PAGE), jnp.float32),
            pltpu.VMEM((block, cached), jnp.float32),
            pltpu.VMEM((kvh, count, own, HD), jnp.bfloat16),
            pltpu.VMEM((kvh, count, 1, own), jnp.float32),
            pltpu.VMEM((kvh, count, own, HD), jnp.bfloat16),
            pltpu.VMEM((kvh, count, 1, own), jnp.float32),
            pltpu.VMEM((HD, own), jnp.float32),
            dma((5,)),
            dma((kvh,)),
            dma((kvh,)),
            dma((kvh, count - 1)),
            dma((kvh, count - 1)),
            dma((kvh, count - 1)),
            dma((kvh, count - 1)),
            dma((kvh, count - 1)),
            dma((kvh, count - 1)),
        ],
        compiler_params=pltpu.CompilerParams(
            collective_id=0, has_side_effects=True, vmem_limit_bytes=60 * 1024 * 1024
        ),
        cost_estimate=pl.CostEstimate(
            flops=4 * count * rows * heads * cached * HD,
            bytes_accessed=4 * cached * kvh * HD,
            transcendentals=count * rows * heads * cached,
        ),
        name="paged_attention",
    )(
        queries.reshape(rows, heads, HD).transpose(1, 0, 2).reshape(kvh, own, HD),
        new_keys.reshape(rows, kvh, HD).transpose(1, 0, 2),
        new_values.reshape(rows, kvh, HD).transpose(1, 0, 2),
        cache_keys,
        cache_values,
        cache_length,
        page_table.reshape(1, -1),
    )
    return out.reshape(heads, rows, HD).transpose(1, 0, 2).reshape(rows, width)


def solution(mesh):
    in_specs = (
        P(("req", "ctx"), None),
        P(("req", "ctx"), None),
        P(("req", "ctx"), None),
        P(("req", "ctx"), None),
        P(("req", "ctx"), None),
        P("req"),
        P("req"),
    )
    out_specs = P(("req", "ctx"), None)
    return jax.shard_map(local, mesh=mesh, in_specs=in_specs, out_specs=out_specs, check_vma=False)
```

```python
import functools
import math

import jax
import jax.numpy as jnp
from jax import lax
from jax.experimental import pallas as pl
from jax.experimental.pallas import tpu as pltpu
from jax.sharding import PartitionSpec as P

HD = 128
PAGE = 128
FLOOR = -1e30
BLOCK = 256
ROWS = 256


def kernel(
    count,
    q_ref,
    new_k_ref,
    new_v_ref,
    cache_k_ref,
    cache_v_ref,
    length_ref,
    table_ref,
    out_ref,
    new_k,
    new_v,
    length_at,
    table,
    tail,
    q_all,
    k_buf,
    v_buf,
    bias,
    bias_new,
    scores,
    part,
    stat,
    part_in,
    stat_in,
    weigh,
    small_sem,
    k_sem,
    v_sem,
    q_send,
    q_recv,
    part_send,
    part_recv,
    stat_send,
    stat_recv,
):
    me = lax.axis_index("ctx")
    kvh, own, _ = q_ref.shape
    rows = new_k_ref.shape[1]
    cached = cache_k_ref.shape[0]
    pages = cached // PAGE
    total_rows = count * own
    block = min(ROWS, total_rows)
    scale = HD ** (-0.5) * math.log2(math.e)

    def each_head(body):
        lax.fori_loop(0, kvh, lambda k, carry: (body(k), carry)[1], 0)

    def cache_copy(source, target, sems, k):
        return pltpu.make_async_copy(
            source.at[:, pl.ds(pl.multiple_of(k * HD, HD), HD)], target.at[k, pl.ds(0, cached)], sems.at[k]
        )

    barrier = pltpu.get_barrier_semaphore()
    for off in range(1, count):
        pl.semaphore_signal(
            barrier,
            inc=1,
            device_id={"ctx": lax.rem(me + off, count)},
            device_id_type=pl.DeviceIdType.MESH,
        )
    small = [
        pltpu.make_async_copy(source, target, small_sem.at[i])
        for i, (source, target) in enumerate(
            (
                (new_k_ref, new_k),
                (new_v_ref, new_v),
                (length_ref, length_at),
                (table_ref, table),
            )
        )
    ]
    own_q = pltpu.make_async_copy(q_ref, q_all.at[:, me], small_sem.at[len(small)])
    for copy in small:
        copy.start()
    own_q.start()
    cache_copy(cache_k_ref, k_buf, k_sem, 0).start()
    cache_copy(cache_v_ref, v_buf, v_sem, 0).start()
    pl.semaphore_wait(barrier, count - 1)

    def q_copy(k, off):
        return pltpu.make_async_remote_copy(
            src_ref=q_ref.at[k],
            dst_ref=q_all.at[k, me],
            send_sem=q_send.at[k, off - 1],
            recv_sem=q_recv.at[k, off - 1],
            device_id={"ctx": lax.rem(me + off, count)},
            device_id_type=pl.DeviceIdType.MESH,
        )

    def part_copy(k, off):
        target = lax.rem(me + off, count)
        return pltpu.make_async_remote_copy(
            src_ref=part.at[k, target],
            dst_ref=part_in.at[k, me],
            send_sem=part_send.at[k, off - 1],
            recv_sem=part_recv.at[k, off - 1],
            device_id={"ctx": target},
            device_id_type=pl.DeviceIdType.MESH,
        )

    def stat_copy(k, off):
        target = lax.rem(me + off, count)
        return pltpu.make_async_remote_copy(
            src_ref=stat.at[k, target],
            dst_ref=stat_in.at[k, me],
            send_sem=stat_send.at[k, off - 1],
            recv_sem=stat_recv.at[k, off - 1],
            device_id={"ctx": target},
            device_id_type=pl.DeviceIdType.MESH,
        )

    @each_head
    def _(k):
        for off in range(1, count):
            q_copy(k, off).start()

    @functools.partial(lax.fori_loop, 1, kvh, init_val=0)
    def _(k, carry):
        cache_copy(cache_k_ref, k_buf, k_sem, k).start()
        cache_copy(cache_v_ref, v_buf, v_sem, k).start()
        return carry


    for copy in small:
        copy.wait()
    tail[...] = jnp.zeros_like(tail)
    @each_head
    def _(k):
        tail[0:rows, :] = new_k[k].astype(jnp.float32)
        k_buf[k, cached:, :] = tail[...].astype(jnp.bfloat16)
        tail[0:rows, :] = new_v[k].astype(jnp.float32)
        v_buf[k, cached:, :] = tail[...].astype(jnp.bfloat16)

    length = length_at[0]
    slots = me * pages + lax.broadcasted_iota(jnp.int32, (pages, table.shape[1]), 0)
    order = lax.broadcasted_iota(jnp.int32, (pages, table.shape[1]), 1)
    hits = jnp.where(table[...] == slots, order, 0)
    logical = jnp.sum(hits, axis=1, keepdims=True)
    lane = lax.broadcasted_iota(jnp.int32, (pages, PAGE), 1)
    bias[...] = jnp.where(logical * PAGE + lane < length, 0.0, FLOOR)

    token = lax.rem(lax.broadcasted_iota(jnp.int32, (own, PAGE), 0), rows)
    column = lax.broadcasted_iota(jnp.int32, (own, PAGE), 1)
    first = jnp.where(column < rows, me * rows + column - token, count * rows)
    for s in range(count):
        bias_new[s] = jnp.where(first <= s * rows, 0.0, FLOOR)

    spans = [(at, min(BLOCK, cached - at)) for at in range(0, cached, BLOCK)]

    def attend(k, at):
        if total_rows == block:
            query = q_all[k].reshape(total_rows, HD)
        else:
            parts = block // own
            query = q_all[k, pl.ds(at * parts, parts)].reshape(block, HD)
        top = None
        for start, size in spans:
            score = lax.dot_general(
                query,
                k_buf[k, start : start + size, :],
                (((1,), (1,)), ((), ())),
                preferred_element_type=jnp.float32,
            )
            for page in range(size // PAGE):
                j = start // PAGE + page
                tile = score[:, page * PAGE : (page + 1) * PAGE] * scale + bias[j : j + 1, :]
                scores[:, j * PAGE : (j + 1) * PAGE] = tile
                top = tile if top is None else jnp.maximum(top, tile)
        score = lax.dot_general(
            query,
            k_buf[k, cached:, :],
            (((1,), (1,)), ((), ())),
            preferred_element_type=jnp.float32,
        )
        barred = bias_new[pl.ds(at * (block // own), block // own)].reshape(block, PAGE)
        last = score * scale + barred
        top = jnp.max(jnp.maximum(top, last), axis=1, keepdims=True)
        weight = jnp.exp2(last - top)
        summed = weight
        mixed = jnp.dot(
            weight.astype(jnp.bfloat16), v_buf[k, cached:, :], preferred_element_type=jnp.float32
        )
        for start, size in spans:
            weight = jnp.exp2(scores[:, start : start + size] - top)
            for page in range(size // PAGE):
                summed = summed + weight[:, page * PAGE : (page + 1) * PAGE]
            mixed = mixed + jnp.dot(
                weight.astype(jnp.bfloat16),
                v_buf[k, start : start + size, :],
                preferred_element_type=jnp.float32,
            )
        total = jnp.sum(summed, axis=1, keepdims=True)
        mixed = mixed * (1.0 / total)
        level = top + jnp.log(total) * math.log2(math.e)
        lanes = lax.broadcasted_iota(jnp.int32, (own, HD), 1)
        columns = jnp.zeros((own, HD), jnp.float32)
        for i in range(block // own):
            piece = slice(i * own, (i + 1) * own)
            part[k, at * (block // own) + i] = mixed[piece].astype(jnp.bfloat16)
            columns = jnp.where(lanes == i, level[piece], columns)
        turned = columns.T
        for i in range(block // own):
            stat[k, at * (block // own) + i] = turned[i : i + 1, :]

    own_q.wait()

    def one_head(k, carry):
        for off in range(1, count):
            q_copy(k, off).wait_recv()
        cache_copy(cache_k_ref, k_buf, k_sem, k).wait()
        cache_copy(cache_v_ref, v_buf, v_sem, k).wait()
        if total_rows == block:
            attend(k, 0)
        else:
            lax.fori_loop(0, total_rows // block, lambda at, c: (attend(k, at), c)[1], 0)
        for off in range(1, count):
            part_copy(k, off).start()
            stat_copy(k, off).start()
        part_in[k, me] = part[k, me]
        stat_in[k, me] = stat[k, me]
        return carry

    lax.fori_loop(0, kvh, one_head, 0)

    def combine(k, carry):
        for off in range(1, count):
            part_copy(k, off).wait_recv()
            stat_copy(k, off).wait_recv()
        for off in range(1, count):
            q_copy(k, off).wait_send()
            part_copy(k, off).wait_send()
            stat_copy(k, off).wait_send()
        levels = [stat_in[k, s] for s in range(count)]
        top = functools.reduce(jnp.maximum, levels)
        shares = [jnp.exp2(level - top) for level in levels]
        share = 1.0 / functools.reduce(jnp.add, shares)
        for s in range(count):
            weigh[s : s + 1, :] = shares[s] * share
        turned = weigh[...].T
        result = jnp.zeros((own, HD), jnp.float32)
        for s in range(count):
            result = result + part_in[k, s].astype(jnp.float32) * turned[:, s : s + 1]
        out_ref[k] = result.astype(out_ref.dtype)
        return carry

    weigh[...] = jnp.zeros_like(weigh)
    lax.fori_loop(0, kvh, combine, 0)


def local(queries, new_keys, new_values, cache_keys, cache_values, cache_length, page_table):
    count = lax.axis_size("ctx")
    rows, width = queries.shape
    heads = width // HD
    cached = cache_keys.shape[0]
    kvh = cache_keys.shape[1] // HD
    group = heads // kvh
    own = rows * group
    block = min(ROWS, count * own)
    pages = cached // PAGE
    vmem = pl.BlockSpec(memory_space=pltpu.VMEM)
    held = pl.BlockSpec(memory_space=pltpu.HBM)
    dma = pltpu.SemaphoreType.DMA
    out = pl.pallas_call(
        functools.partial(kernel, count),
        out_shape=pltpu.VMEM((kvh, own, HD), jnp.bfloat16),
        in_specs=[held] * 7,
        out_specs=vmem,
        scratch_shapes=[
            pltpu.VMEM((kvh, rows, HD), jnp.bfloat16),
            pltpu.VMEM((kvh, rows, HD), jnp.bfloat16),
            pltpu.SMEM((1,), jnp.int32),
            pltpu.VMEM((1, page_table.shape[0]), jnp.int32),
            pltpu.VMEM((PAGE, HD), jnp.float32),
            pltpu.VMEM((kvh, count, own, HD), jnp.bfloat16),
            pltpu.VMEM((kvh, cached + PAGE, HD), jnp.bfloat16),
            pltpu.VMEM((kvh, cached + PAGE, HD), jnp.bfloat16),
            pltpu.VMEM((pages, PAGE), jnp.float32),
            pltpu.VMEM((count, own, PAGE), jnp.float32),
            pltpu.VMEM((block, cached), jnp.float32),
            pltpu.VMEM((kvh, count, own, HD), jnp.bfloat16),
            pltpu.VMEM((kvh, count, 1, own), jnp.float32),
            pltpu.VMEM((kvh, count, own, HD), jnp.bfloat16),
            pltpu.VMEM((kvh, count, 1, own), jnp.float32),
            pltpu.VMEM((HD, own), jnp.float32),
            dma((5,)),
            dma((kvh,)),
            dma((kvh,)),
            dma((kvh, count - 1)),
            dma((kvh, count - 1)),
            dma((kvh, count - 1)),
            dma((kvh, count - 1)),
            dma((kvh, count - 1)),
            dma((kvh, count - 1)),
        ],
        compiler_params=pltpu.CompilerParams(
            collective_id=0, has_side_effects=True, vmem_limit_bytes=60 * 1024 * 1024
        ),
        cost_estimate=pl.CostEstimate(
            flops=4 * count * rows * heads * cached * HD,
            bytes_accessed=4 * cached * kvh * HD,
            transcendentals=count * rows * heads * cached,
        ),
        name="paged_attention",
    )(
        queries.reshape(rows, heads, HD).transpose(1, 0, 2).reshape(kvh, own, HD),
        new_keys.reshape(rows, kvh, HD).transpose(1, 0, 2),
        new_values.reshape(rows, kvh, HD).transpose(1, 0, 2),
        cache_keys,
        cache_values,
        cache_length,
        page_table.reshape(1, -1),
    )
    return out.reshape(heads, rows, HD).transpose(1, 0, 2).reshape(rows, width)


def solution(mesh):
    in_specs = (
        P(("req", "ctx"), None),
        P(("req", "ctx"), None),
        P(("req", "ctx"), None),
        P(("req", "ctx"), None),
        P(("req", "ctx"), None),
        P("req"),
        P("req"),
    )
    out_specs = P(("req", "ctx"), None)
    return jax.shard_map(local, mesh=mesh, in_specs=in_specs, out_specs=out_specs, check_vma=False)
```

```python
import functools
import math

import jax
import jax.numpy as jnp
from jax import lax
from jax.experimental import pallas as pl
from jax.experimental.pallas import tpu as pltpu
from jax.sharding import PartitionSpec as P

HD = 128
PAGE = 128
FLOOR = -1e30
BLOCK = 256
ROWS = 256


def kernel(
    count,
    q_ref,
    new_k_ref,
    new_v_ref,
    cache_k_ref,
    cache_v_ref,
    length_ref,
    table_ref,
    out_ref,
    new_k,
    new_v,
    length_at,
    table,
    tail,
    q_all,
    k_buf,
    v_buf,
    bias,
    bias_new,
    scores,
    weights,
    part,
    stat,
    part_in,
    stat_in,
    weigh,
    small_sem,
    k_sem,
    v_sem,
    q_send,
    q_recv,
    part_send,
    part_recv,
    stat_send,
    stat_recv,
):
    me = lax.axis_index("ctx")
    kvh, own, _ = q_ref.shape
    rows = new_k_ref.shape[1]
    cached = cache_k_ref.shape[0]
    pages = cached // PAGE
    total_rows = count * own
    block = min(ROWS, total_rows)
    scale = HD ** (-0.5) * math.log2(math.e)

    def each_head(body):
        lax.fori_loop(0, kvh, lambda k, carry: (body(k), carry)[1], 0)

    def cache_copy(source, target, sems, k):
        return pltpu.make_async_copy(
            source.at[:, pl.ds(pl.multiple_of(k * HD, HD), HD)], target.at[k, pl.ds(0, cached)], sems.at[k]
        )

    barrier = pltpu.get_barrier_semaphore()
    for off in range(1, count):
        pl.semaphore_signal(
            barrier,
            inc=1,
            device_id={"ctx": lax.rem(me + off, count)},
            device_id_type=pl.DeviceIdType.MESH,
        )
    small = [
        pltpu.make_async_copy(source, target, small_sem.at[i])
        for i, (source, target) in enumerate(
            (
                (new_k_ref, new_k),
                (new_v_ref, new_v),
                (length_ref, length_at),
                (table_ref, table),
            )
        )
    ]
    own_q = pltpu.make_async_copy(q_ref, q_all.at[:, me], small_sem.at[len(small)])
    for copy in small:
        copy.start()
    own_q.start()
    cache_copy(cache_k_ref, k_buf, k_sem, 0).start()
    cache_copy(cache_v_ref, v_buf, v_sem, 0).start()
    pl.semaphore_wait(barrier, count - 1)

    def q_copy(k, off):
        return pltpu.make_async_remote_copy(
            src_ref=q_ref.at[k],
            dst_ref=q_all.at[k, me],
            send_sem=q_send.at[k, off - 1],
            recv_sem=q_recv.at[k, off - 1],
            device_id={"ctx": lax.rem(me + off, count)},
            device_id_type=pl.DeviceIdType.MESH,
        )

    def part_copy(k, off):
        target = lax.rem(me + off, count)
        return pltpu.make_async_remote_copy(
            src_ref=part.at[k, target],
            dst_ref=part_in.at[k, me],
            send_sem=part_send.at[k, off - 1],
            recv_sem=part_recv.at[k, off - 1],
            device_id={"ctx": target},
            device_id_type=pl.DeviceIdType.MESH,
        )

    def stat_copy(k, off):
        target = lax.rem(me + off, count)
        return pltpu.make_async_remote_copy(
            src_ref=stat.at[k, target],
            dst_ref=stat_in.at[k, me],
            send_sem=stat_send.at[k, off - 1],
            recv_sem=stat_recv.at[k, off - 1],
            device_id={"ctx": target},
            device_id_type=pl.DeviceIdType.MESH,
        )

    @each_head
    def _(k):
        for off in range(1, count):
            q_copy(k, off).start()

    @functools.partial(lax.fori_loop, 1, kvh, init_val=0)
    def _(k, carry):
        cache_copy(cache_k_ref, k_buf, k_sem, k).start()
        cache_copy(cache_v_ref, v_buf, v_sem, k).start()
        return carry


    for copy in small:
        copy.wait()
    tail[...] = jnp.zeros_like(tail)
    @each_head
    def _(k):
        tail[0:rows, :] = new_k[k].astype(jnp.float32)
        k_buf[k, cached:, :] = tail[...].astype(jnp.bfloat16)
        tail[0:rows, :] = new_v[k].astype(jnp.float32)
        v_buf[k, cached:, :] = tail[...].astype(jnp.bfloat16)

    length = length_at[0]
    slots = me * pages + lax.broadcasted_iota(jnp.int32, (pages, table.shape[1]), 0)
    order = lax.broadcasted_iota(jnp.int32, (pages, table.shape[1]), 1)
    hits = jnp.where(table[...] == slots, order, 0)
    logical = jnp.sum(hits, axis=1, keepdims=True)
    lane = lax.broadcasted_iota(jnp.int32, (pages, PAGE), 1)
    bias[...] = jnp.where(logical * PAGE + lane < length, 0.0, FLOOR)

    token = lax.rem(lax.broadcasted_iota(jnp.int32, (own, PAGE), 0), rows)
    column = lax.broadcasted_iota(jnp.int32, (own, PAGE), 1)
    first = jnp.where(column < rows, me * rows + column - token, count * rows)
    for s in range(count):
        bias_new[s] = jnp.where(first <= s * rows, 0.0, FLOOR)

    spans = [(at, min(BLOCK, cached - at)) for at in range(0, cached, BLOCK)]

    def attend(k, at):
        if total_rows == block:
            query = q_all[k].reshape(total_rows, HD)
        else:
            parts = block // own
            query = q_all[k, pl.ds(at * parts, parts)].reshape(block, HD)
        top = None
        for start, size in spans:
            score = lax.dot_general(
                query,
                k_buf[k, start : start + size, :],
                (((1,), (1,)), ((), ())),
                preferred_element_type=jnp.float32,
            )
            for page in range(size // PAGE):
                j = start // PAGE + page
                tile = score[:, page * PAGE : (page + 1) * PAGE] * scale + bias[j : j + 1, :]
                scores[:, j * PAGE : (j + 1) * PAGE] = tile
                top = tile if top is None else jnp.maximum(top, tile)
        score = lax.dot_general(
            query,
            k_buf[k, cached:, :],
            (((1,), (1,)), ((), ())),
            preferred_element_type=jnp.float32,
        )
        barred = bias_new[pl.ds(at * (block // own), block // own)].reshape(block, PAGE)
        last = score * scale + barred
        top = jnp.max(jnp.maximum(top, last), axis=1, keepdims=True)
        weight = jnp.exp2(last - top)
        weights[:, cached:] = weight.astype(jnp.bfloat16)
        summed = weight
        for start, size in spans:
            weight = jnp.exp2(scores[:, start : start + size] - top)
            for page in range(size // PAGE):
                summed = summed + weight[:, page * PAGE : (page + 1) * PAGE]
            weights[:, start : start + size] = weight.astype(jnp.bfloat16)
        mixed = jnp.dot(weights[...], v_buf[k], preferred_element_type=jnp.float32)
        total = jnp.sum(summed, axis=1, keepdims=True)
        mixed = mixed * (1.0 / total)
        level = top + jnp.log(total) * math.log2(math.e)
        lanes = lax.broadcasted_iota(jnp.int32, (own, HD), 1)
        columns = jnp.zeros((own, HD), jnp.float32)
        for i in range(block // own):
            piece = slice(i * own, (i + 1) * own)
            part[k, at * (block // own) + i] = mixed[piece].astype(jnp.bfloat16)
            columns = jnp.where(lanes == i, level[piece], columns)
        turned = columns.T
        for i in range(block // own):
            stat[k, at * (block // own) + i] = turned[i : i + 1, :]

    own_q.wait()

    def one_head(k, carry):
        for off in range(1, count):
            q_copy(k, off).wait_recv()
        cache_copy(cache_k_ref, k_buf, k_sem, k).wait()
        cache_copy(cache_v_ref, v_buf, v_sem, k).wait()
        if total_rows == block:
            attend(k, 0)
        else:
            lax.fori_loop(0, total_rows // block, lambda at, c: (attend(k, at), c)[1], 0)
        for off in range(1, count):
            part_copy(k, off).start()
            stat_copy(k, off).start()
        part_in[k, me] = part[k, me]
        stat_in[k, me] = stat[k, me]
        return carry

    lax.fori_loop(0, kvh, one_head, 0)

    def combine(k, carry):
        for off in range(1, count):
            part_copy(k, off).wait_recv()
            stat_copy(k, off).wait_recv()
        for off in range(1, count):
            q_copy(k, off).wait_send()
            part_copy(k, off).wait_send()
            stat_copy(k, off).wait_send()
        levels = [stat_in[k, s] for s in range(count)]
        top = functools.reduce(jnp.maximum, levels)
        shares = [jnp.exp2(level - top) for level in levels]
        share = 1.0 / functools.reduce(jnp.add, shares)
        for s in range(count):
            weigh[s : s + 1, :] = shares[s] * share
        turned = weigh[...].T
        result = jnp.zeros((own, HD), jnp.float32)
        for s in range(count):
            result = result + part_in[k, s].astype(jnp.float32) * turned[:, s : s + 1]
        out_ref[k] = result.astype(out_ref.dtype)
        return carry

    weigh[...] = jnp.zeros_like(weigh)
    lax.fori_loop(0, kvh, combine, 0)


def local(queries, new_keys, new_values, cache_keys, cache_values, cache_length, page_table):
    count = lax.axis_size("ctx")
    rows, width = queries.shape
    heads = width // HD
    cached = cache_keys.shape[0]
    kvh = cache_keys.shape[1] // HD
    group = heads // kvh
    own = rows * group
    block = min(ROWS, count * own)
    pages = cached // PAGE
    vmem = pl.BlockSpec(memory_space=pltpu.VMEM)
    held = pl.BlockSpec(memory_space=pltpu.HBM)
    dma = pltpu.SemaphoreType.DMA
    out = pl.pallas_call(
        functools.partial(kernel, count),
        out_shape=pltpu.VMEM((kvh, own, HD), jnp.bfloat16),
        in_specs=[held] * 7,
        out_specs=vmem,
        scratch_shapes=[
            pltpu.VMEM((kvh, rows, HD), jnp.bfloat16),
            pltpu.VMEM((kvh, rows, HD), jnp.bfloat16),
            pltpu.SMEM((1,), jnp.int32),
            pltpu.VMEM((1, page_table.shape[0]), jnp.int32),
            pltpu.VMEM((PAGE, HD), jnp.float32),
            pltpu.VMEM((kvh, count, own, HD), jnp.bfloat16),
            pltpu.VMEM((kvh, cached + PAGE, HD), jnp.bfloat16),
            pltpu.VMEM((kvh, cached + PAGE, HD), jnp.bfloat16),
            pltpu.VMEM((pages, PAGE), jnp.float32),
            pltpu.VMEM((count, own, PAGE), jnp.float32),
            pltpu.VMEM((block, cached), jnp.float32),
            pltpu.VMEM((block, cached + PAGE), jnp.bfloat16),
            pltpu.VMEM((kvh, count, own, HD), jnp.bfloat16),
            pltpu.VMEM((kvh, count, 1, own), jnp.float32),
            pltpu.VMEM((kvh, count, own, HD), jnp.bfloat16),
            pltpu.VMEM((kvh, count, 1, own), jnp.float32),
            pltpu.VMEM((HD, own), jnp.float32),
            dma((5,)),
            dma((kvh,)),
            dma((kvh,)),
            dma((kvh, count - 1)),
            dma((kvh, count - 1)),
            dma((kvh, count - 1)),
            dma((kvh, count - 1)),
            dma((kvh, count - 1)),
            dma((kvh, count - 1)),
        ],
        compiler_params=pltpu.CompilerParams(
            collective_id=0, has_side_effects=True, vmem_limit_bytes=60 * 1024 * 1024
        ),
        cost_estimate=pl.CostEstimate(
            flops=4 * count * rows * heads * cached * HD,
            bytes_accessed=4 * cached * kvh * HD,
            transcendentals=count * rows * heads * cached,
        ),
        name="paged_attention",
    )(
        queries.reshape(rows, heads, HD).transpose(1, 0, 2).reshape(kvh, own, HD),
        new_keys.reshape(rows, kvh, HD).transpose(1, 0, 2),
        new_values.reshape(rows, kvh, HD).transpose(1, 0, 2),
        cache_keys,
        cache_values,
        cache_length,
        page_table.reshape(1, -1),
    )
    return out.reshape(heads, rows, HD).transpose(1, 0, 2).reshape(rows, width)


def solution(mesh):
    in_specs = (
        P(("req", "ctx"), None),
        P(("req", "ctx"), None),
        P(("req", "ctx"), None),
        P(("req", "ctx"), None),
        P(("req", "ctx"), None),
        P("req"),
        P("req"),
    )
    out_specs = P(("req", "ctx"), None)
    return jax.shard_map(local, mesh=mesh, in_specs=in_specs, out_specs=out_specs, check_vma=False)
```

```python
import functools
import math

import jax
import jax.numpy as jnp
from jax import lax
from jax.experimental import pallas as pl
from jax.experimental.pallas import tpu as pltpu
from jax.sharding import PartitionSpec as P

HD = 128
PAGE = 128
FLOOR = -1e30
BLOCK = 256


def kernel(
    count,
    q_ref,
    new_k_ref,
    new_v_ref,
    cache_k_ref,
    cache_v_ref,
    length_ref,
    table_ref,
    out_ref,
    new_k,
    new_v,
    length_at,
    table,
    tail,
    q_all,
    k_buf,
    v_buf,
    bias,
    scores,
    part,
    stat,
    part_in,
    stat_in,
    weigh,
    small_sem,
    k_sem,
    v_sem,
    q_send,
    q_recv,
    far_send,
    far_recv,
    cross_send,
    cross_recv,
    pass_send,
    pass_recv,
    part_send,
    part_recv,
    stat_send,
    stat_recv,
):
    me = lax.axis_index("ctx")
    kvh, own, _ = q_ref.shape
    rows = new_k_ref.shape[1]
    cached = cache_k_ref.shape[0]
    pages = cached // PAGE
    total_rows = count * own
    block = min(BLOCK, total_rows)
    scale = HD ** (-0.5) * math.log2(math.e)

    def cache_copy(source, target, sems, k):
        return pltpu.make_async_copy(
            source.at[:, pl.ds(k * HD, HD)], target.at[k, pl.ds(0, cached)], sems.at[k]
        )

    barrier = pltpu.get_barrier_semaphore()
    for off in range(1, count):
        pl.semaphore_signal(
            barrier,
            inc=1,
            device_id={"ctx": lax.rem(me + off, count)},
            device_id_type=pl.DeviceIdType.MESH,
        )
    small = [
        pltpu.make_async_copy(source, target, small_sem.at[i])
        for i, (source, target) in enumerate(
            (
                (new_k_ref, new_k),
                (new_v_ref, new_v),
                (length_ref, length_at),
                (table_ref, table),
            )
        )
    ]
    own_q = pltpu.make_async_copy(q_ref, q_all.at[:, me], small_sem.at[len(small)])
    for copy in small:
        copy.start()
    own_q.start()
    for k in range(kvh):
        cache_copy(cache_k_ref, k_buf, k_sem, k).start()
        cache_copy(cache_v_ref, v_buf, v_sem, k).start()
    pl.semaphore_wait(barrier, count - 1)

    halves = 2 if count % 2 == 0 else 1
    half = count // halves
    side = me // half
    base = side * half
    other = (halves - 1 - side) * half
    relay = me == half - 1 + side

    def near(off):
        return base + lax.rem(me - base + off, half)

    def q_copy(k, off):
        return pltpu.make_async_remote_copy(
            src_ref=q_ref.at[k],
            dst_ref=q_all.at[k, me],
            send_sem=q_send.at[k, off - 1],
            recv_sem=q_recv.at[k, off - 1],
            device_id={"ctx": near(off)},
            device_id_type=pl.DeviceIdType.MESH,
        )

    def far_copy(target, slot):
        return pltpu.make_async_remote_copy(
            src_ref=q_ref.at[0],
            dst_ref=q_all.at[0, me],
            send_sem=far_send.at[target],
            recv_sem=far_recv.at[slot],
            device_id={"ctx": other + target},
            device_id_type=pl.DeviceIdType.MESH,
        )

    def cross_copy(k, slot):
        return pltpu.make_async_remote_copy(
            src_ref=q_ref.at[k],
            dst_ref=q_all.at[k, me],
            send_sem=cross_send.at[k],
            recv_sem=cross_recv.at[k, slot],
            device_id={"ctx": half - side},
            device_id_type=pl.DeviceIdType.MESH,
        )

    def pass_copy(k, off):
        return pltpu.make_async_remote_copy(
            src_ref=q_all.at[k, pl.ds(other, half)],
            dst_ref=q_all.at[k, pl.ds(other, half)],
            send_sem=pass_send.at[k, off - 1],
            recv_sem=pass_recv.at[k],
            device_id={"ctx": near(off)},
            device_id_type=pl.DeviceIdType.MESH,
        )

    def pass_on(k):
        for slot in range(half):
            cross_copy(k, slot).wait_recv()
        for off in range(1, half):
            pass_copy(k, off).start()

    def part_copy(k, off):
        target = lax.rem(me + off, count)
        return pltpu.make_async_remote_copy(
            src_ref=part.at[k, target],
            dst_ref=part_in.at[k, me],
            send_sem=part_send.at[k, off - 1],
            recv_sem=part_recv.at[k, off - 1],
            device_id={"ctx": target},
            device_id_type=pl.DeviceIdType.MESH,
        )

    def stat_copy(k, off):
        target = lax.rem(me + off, count)
        return pltpu.make_async_remote_copy(
            src_ref=stat.at[k, target],
            dst_ref=stat_in.at[k, me],
            send_sem=stat_send.at[k, off - 1],
            recv_sem=stat_recv.at[k, off - 1],
            device_id={"ctx": target},
            device_id_type=pl.DeviceIdType.MESH,
        )

    for k in range(kvh):
        if halves == 2 and k == 0:
            for target in range(half):
                far_copy(target, me - base).start()
        elif halves == 2:
            cross_copy(k, me - base).start()
        for off in range(1, half):
            q_copy(k, off).start()

    for copy in small:
        copy.wait()
    tail[...] = jnp.zeros_like(tail)
    for k in range(kvh):
        tail[0:rows, :] = new_k[k].astype(jnp.float32)
        k_buf[k, cached:, :] = tail[...].astype(jnp.bfloat16)
        tail[0:rows, :] = new_v[k].astype(jnp.float32)
        v_buf[k, cached:, :] = tail[...].astype(jnp.bfloat16)

    length = length_at[0]
    slots = me * pages + lax.broadcasted_iota(jnp.int32, (pages, table.shape[1]), 0)
    order = lax.broadcasted_iota(jnp.int32, (pages, table.shape[1]), 1)
    hits = jnp.where(table[...] == slots, order, 0)
    logical = jnp.sum(hits, axis=1, keepdims=True)
    lane = lax.broadcasted_iota(jnp.int32, (pages, PAGE), 1)
    bias[...] = jnp.where(logical * PAGE + lane < length, 0.0, FLOOR)

    spans = [(at, min(BLOCK, cached - at)) for at in range(0, cached, BLOCK)]

    def attend(k, at, between=None):
        if total_rows == block:
            query = q_all[k].reshape(total_rows, HD)
        else:
            parts = block // own
            query = q_all[k, pl.ds(at * parts, parts)].reshape(block, HD)
        top = None
        for start, size in spans:
            score = lax.dot_general(
                query,
                k_buf[k, start : start + size, :],
                (((1,), (1,)), ((), ())),
                preferred_element_type=jnp.float32,
            )
            for page in range(size // PAGE):
                j = start // PAGE + page
                tile = score[:, page * PAGE : (page + 1) * PAGE] * scale + bias[j : j + 1, :]
                scores[:, j * PAGE : (j + 1) * PAGE] = tile
                top = tile if top is None else jnp.maximum(top, tile)
        score = lax.dot_general(
            query,
            k_buf[k, cached:, :],
            (((1,), (1,)), ((), ())),
            preferred_element_type=jnp.float32,
        )
        if between is not None:
            between()
        row = at * block + lax.broadcasted_iota(jnp.int32, (block, PAGE), 0)
        column = lax.broadcasted_iota(jnp.int32, (block, PAGE), 1)
        token = (row // own) * rows + row % rows
        allowed = (column < rows) & (me * rows + column <= token)
        last = jnp.where(allowed, score * scale, FLOOR)
        top = jnp.max(jnp.maximum(top, last), axis=1, keepdims=True)
        weight = jnp.exp2(last - top)
        summed = weight
        mixed = jnp.dot(
            weight.astype(jnp.bfloat16), v_buf[k, cached:, :], preferred_element_type=jnp.float32
        )
        for start, size in spans:
            weight = jnp.exp2(scores[:, start : start + size] - top)
            for page in range(size // PAGE):
                summed = summed + weight[:, page * PAGE : (page + 1) * PAGE]
            mixed = mixed + jnp.dot(
                weight.astype(jnp.bfloat16),
                v_buf[k, start : start + size, :],
                preferred_element_type=jnp.float32,
            )
        total = jnp.sum(summed, axis=1, keepdims=True)
        mixed = mixed * (1.0 / total)
        lanes = lax.broadcasted_iota(jnp.int32, (2 * own, 128), 1)
        columns = jnp.zeros((2 * own, 128), jnp.float32)
        for i in range(block // own):
            piece = slice(i * own, (i + 1) * own)
            slot = at * (block // own) + i
            part[k, slot] = mixed[piece].astype(jnp.bfloat16)
            column = jnp.concatenate([top[piece], total[piece]], axis=0)
            columns = jnp.where(lanes == i, column, columns)
        turned = columns.T
        for i in range(block // own):
            stat[k, at * (block // own) + i] = turned[i : i + 1, :]

    own_q.wait()

    def pass_next(k):
        if halves == 2:
            pl.when(relay & (k + 1 < kvh))(lambda: pass_on(k + 1))

    def one_head(k, carry):
        for off in range(1, half):
            q_copy(k, off).wait_recv()
        if halves == 2:

            @pl.when(k == 0)
            def _():
                for slot in range(half):
                    far_copy(0, slot).wait_recv()

        if halves == 2 and half > 1:

            @pl.when(jnp.logical_not(relay) & (k > 0))
            def _():
                pass_copy(k, 1).wait_recv()

        cache_copy(cache_k_ref, k_buf, k_sem, k).wait()
        cache_copy(cache_v_ref, v_buf, v_sem, k).wait()
        if total_rows == block:
            attend(k, 0, lambda: pass_next(k))
        else:
            pass_next(k)
            lax.fori_loop(0, total_rows // block, lambda at, c: (attend(k, at), c)[1], 0)
        for off in range(1, count):
            part_copy(k, off).start()
            stat_copy(k, off).start()
        part_in[k, me] = part[k, me]
        stat_in[k, me] = stat[k, me]
        return carry

    lax.fori_loop(0, kvh, one_head, 0)

    def combine(k, carry):
        for off in range(1, count):
            part_copy(k, off).wait_recv()
            stat_copy(k, off).wait_recv()
        tops = [stat_in[k, s] for s in range(count)]
        totals = [pltpu.roll(t, own, 1) for t in tops]
        top = functools.reduce(jnp.maximum, tops)
        shares = [jnp.exp2(t - top) * l for t, l in zip(tops, totals)]
        share = 1.0 / functools.reduce(jnp.add, shares)
        for s in range(count):
            weigh[s : s + 1, :] = shares[s] * share
        turned = weigh[...].T
        result = jnp.zeros((own, HD), jnp.float32)
        for s in range(count):
            result = result + part_in[k, s].astype(jnp.float32) * turned[0:own, s : s + 1]
        out_ref[k] = result.astype(out_ref.dtype)
        return carry

    weigh[...] = jnp.zeros_like(weigh)
    lax.fori_loop(0, kvh, combine, 0)

    for k in range(kvh):
        for off in range(1, half):
            q_copy(k, off).wait_send()
        for off in range(1, count):
            part_copy(k, off).wait_send()
            stat_copy(k, off).wait_send()
    if halves == 2:
        for target in range(half):
            far_copy(target, 0).wait_send()
        for k in range(1, kvh):
            cross_copy(k, 0).wait_send()

        @pl.when(relay)
        def _():
            for k in range(1, kvh):
                for off in range(1, half):
                    pass_copy(k, off).wait_send()


def local(queries, new_keys, new_values, cache_keys, cache_values, cache_length, page_table):
    count = lax.axis_size("ctx")
    rows, width = queries.shape
    heads = width // HD
    cached = cache_keys.shape[0]
    kvh = cache_keys.shape[1] // HD
    group = heads // kvh
    own = rows * group
    block = min(BLOCK, count * own)
    pages = cached // PAGE
    half = count // 2 if count % 2 == 0 else count
    vmem = pl.BlockSpec(memory_space=pltpu.VMEM)
    held = pl.BlockSpec(memory_space=pltpu.HBM)
    dma = pltpu.SemaphoreType.DMA
    out = pl.pallas_call(
        functools.partial(kernel, count),
        out_shape=pltpu.VMEM((kvh, own, HD), jnp.bfloat16),
        in_specs=[held] * 7,
        out_specs=vmem,
        scratch_shapes=[
            pltpu.VMEM((kvh, rows, HD), jnp.bfloat16),
            pltpu.VMEM((kvh, rows, HD), jnp.bfloat16),
            pltpu.SMEM((1,), jnp.int32),
            pltpu.VMEM((1, page_table.shape[0]), jnp.int32),
            pltpu.VMEM((PAGE, HD), jnp.float32),
            pltpu.VMEM((kvh, count, own, HD), jnp.bfloat16),
            pltpu.VMEM((kvh, cached + PAGE, HD), jnp.bfloat16),
            pltpu.VMEM((kvh, cached + PAGE, HD), jnp.bfloat16),
            pltpu.VMEM((pages, PAGE), jnp.float32),
            pltpu.VMEM((block, cached), jnp.float32),
            pltpu.VMEM((kvh, count, own, HD), jnp.bfloat16),
            pltpu.VMEM((kvh, count, 1, 2 * own), jnp.float32),
            pltpu.VMEM((kvh, count, own, HD), jnp.bfloat16),
            pltpu.VMEM((kvh, count, 1, 2 * own), jnp.float32),
            pltpu.VMEM((128, 2 * own), jnp.float32),
            dma((5,)),
            dma((kvh,)),
            dma((kvh,)),
            dma((kvh, max(half - 1, 1))),
            dma((kvh, max(half - 1, 1))),
            dma((half,)),
            dma((half,)),
            dma((kvh,)),
            dma((kvh, half)),
            dma((kvh, max(half - 1, 1))),
            dma((kvh,)),
            dma((kvh, count - 1)),
            dma((kvh, count - 1)),
            dma((kvh, count - 1)),
            dma((kvh, count - 1)),
        ],
        compiler_params=pltpu.CompilerParams(
            collective_id=0, has_side_effects=True, vmem_limit_bytes=60 * 1024 * 1024
        ),
        cost_estimate=pl.CostEstimate(
            flops=4 * count * rows * heads * cached * HD,
            bytes_accessed=4 * cached * kvh * HD,
            transcendentals=count * rows * heads * cached,
        ),
        name="paged_attention",
    )(
        queries.reshape(rows, heads, HD).transpose(1, 0, 2).reshape(kvh, own, HD),
        new_keys.reshape(rows, kvh, HD).transpose(1, 0, 2),
        new_values.reshape(rows, kvh, HD).transpose(1, 0, 2),
        cache_keys,
        cache_values,
        cache_length,
        page_table.reshape(1, -1),
    )
    return out.reshape(heads, rows, HD).transpose(1, 0, 2).reshape(rows, width)


def solution(mesh):
    in_specs = (
        P(("req", "ctx"), None),
        P(("req", "ctx"), None),
        P(("req", "ctx"), None),
        P(("req", "ctx"), None),
        P(("req", "ctx"), None),
        P("req"),
        P("req"),
    )
    out_specs = P(("req", "ctx"), None)
    return jax.shard_map(local, mesh=mesh, in_specs=in_specs, out_specs=out_specs, check_vma=False)
```
